256 devices in a mesh: section: 8 (over y, core), fsdp: 32 (over x, z).
Axes of the slice: x: 4, y: 4, z: 8, core: 2. Of those that a mesh axis runs over, the one named last changes fastest.
Arguments:
- grad: bfloat16 [12288, 8192], P(('section', 'fsdp')), parts along dimension 0, may hold values from -40 to 40
- momentum: float32 [12288, 8192], P(('section', 'fsdp')), parts along dimension 0, may hold values from -3 to 3
- left_stat: float32 [24, 32, 256, 512], P('section', 'fsdp'), parts along dimension 0, may hold values from -6 to 6
- right_stat: float32 [24, 32, 256, 512], P('section', 'fsdp'), parts along dimension 0, may hold values from -6 to 6
- left_root: bfloat16 [24, 32, 256, 512], P('section', 'fsdp'), parts along dimension 0, may hold values from -0.25 to 0.25
- right_root: bfloat16 [24, 32, 512, 256], P('section', 'fsdp'), parts along dimension 0, may hold values from -0.25 to 0.25
Outputs:
- new_momentum: float32 [12288, 8192], P(('section', 'fsdp')), parts along dimension 0
- new_left: float32 [24, 32, 256, 512], P('section', 'fsdp'), parts along dimension 0
- new_right: float32 [24, 32, 256, 512], P('section', 'fsdp'), parts along dimension 0
The draws below stay inside these ranges and needn't reach their ends.
There are 8 independent parts, one for each index of `section`. The reference program is written for one: setup_inputs(seed, part) draws one part's arguments, and reference() takes and returns one part's arrays. A program takes and returns all parts, laid end to end along the dimension named above; each array names one. Nothing has to cross between parts.
All inputs are finite; a program needn't handle non-finite values.
Results may differ from the reference program's by a relative error of at most 0.003.
Values may be sent and summed in bfloat16 or wider, within the bound.
No kernel may reach another device: no remote copies, remote signals or barrier semaphores. Data moves between devices by JAX's collectives and lax.ppermute only.
A program may use at most 64 MiB of HBM per device.

```python
import jax
import jax.numpy as jnp
from jax import lax

BLOCK = 512
RB = 3
HALF = 256
ROWS = 1536
COLS = 8192


def draw_grad(key, part):
    key = jax.random.fold_in(key, 11)
    key_base, key_rows, key_cols = jax.random.split(key, 3)
    row_place = jnp.arange(ROWS, dtype=jnp.float32) / ROWS
    col_place = jnp.arange(COLS, dtype=jnp.float32) / COLS
    row_noise = jax.random.uniform(key_rows, (ROWS,), jnp.float32)
    col_noise = jax.random.uniform(key_cols, (COLS,), jnp.float32)
    base = jnp.clip(jax.random.normal(key_base, (ROWS, COLS), jnp.float32), -4.0, 4.0)
    exponent = 0.5 * (row_place + row_noise)[:, None] + 0.5 * (col_place + col_noise)[None, :] - 1.0
    return (base * jnp.power(10.0, exponent)).astype(jnp.bfloat16)


def levels(own_key, dims, cuts, smallest, high):
    def one(position, blocks):
        draws = jax.random.uniform(jax.random.fold_in(jax.random.fold_in(own_key, 6), position), (blocks,), jnp.float32, smallest / len(cuts), high / len(cuts))
        return jnp.repeat(jnp.exp(draws), dims[position] // blocks).reshape((-1,) + (1,) * (len(dims) - position - 1))

    level = one(*cuts[0])
    for cut in cuts[1:]:
        level = level * one(*cut)
    return level


def gaussian(rng, shape, deviation, most, pieces=(), held_as=jnp.bfloat16):
    loudness = levels(rng, shape, pieces, -0.22, 0.18) if pieces else 1.0
    array = jax.random.normal(rng, shape, jnp.float32) * deviation * loudness
    return jnp.minimum(jnp.maximum(array, -most), most).astype(held_as)


def setup_inputs(seed: int = 0, part: int = 0) -> dict:
    arg_keys = jax.random.split(jax.random.key(seed), 7)
    own_keys = jax.random.split(jax.random.fold_in(arg_keys[6], part), 7)
    return {
        "grad": draw_grad(jax.random.fold_in(jax.random.fold_in(arg_keys[6], part), 71), part),
        "momentum": gaussian(own_keys[1], (ROWS, COLS), 0.5, 3.0, ((0, 32),), jnp.float32),
        "left_stat": gaussian(own_keys[2], (RB, 2 * (COLS // BLOCK), HALF, BLOCK), 1.0, 6.0, ((1, 32),), jnp.float32),
        "right_stat": gaussian(own_keys[3], (RB, 2 * (COLS // BLOCK), HALF, BLOCK), 1.0, 6.0, ((1, 32),), jnp.float32),
        "left_root": gaussian(own_keys[4], (RB, 2 * (COLS // BLOCK), HALF, BLOCK), BLOCK ** -0.5, 0.25, ((1, 32),)),
        "right_root": gaussian(own_keys[5], (RB, 2 * (COLS // BLOCK), BLOCK, HALF), BLOCK ** -0.5, 0.25, ((1, 32),)),
    }


decay_stat = 0.95
momentum_rate = 0.9
epsilon = 1e-06

def reference(grad, momentum, left_stat, right_stat, left_root, right_root):
    col_blocks = COLS // BLOCK
    grad_wide = grad.astype(jnp.float32)
    total_sq = jnp.sum(grad_wide * grad_wide)
    clip_limit = 0.5 * jnp.sqrt(jnp.float32(ROWS * COLS))
    clip_factor = jnp.minimum(jnp.float32(1.0), clip_limit / (jnp.sqrt(total_sq) + epsilon))
    blocks = grad.reshape(RB, BLOCK, col_blocks, BLOCK).transpose(0, 2, 1, 3)
    blocks_wide = blocks.astype(jnp.float32)
    left_gram = jnp.einsum('rcik,rcjk->rcij', blocks_wide, blocks_wide)
    right_gram = jnp.einsum('rcki,rckj->rcij', blocks_wide, blocks_wide)
    coeff = (1.0 - decay_stat) * clip_factor * clip_factor
    left_full = left_stat.reshape(RB, col_blocks, BLOCK, BLOCK)
    right_full = right_stat.reshape(RB, col_blocks, BLOCK, BLOCK)
    new_left = decay_stat * left_full + coeff * left_gram
    new_right = decay_stat * right_full + coeff * right_gram
    linv = left_root.reshape(RB, col_blocks, BLOCK, BLOCK).astype(jnp.float32)
    rinv = right_root.reshape(RB, col_blocks, 2, BLOCK, HALF).transpose(0, 1, 3, 2, 4)
    rinv = rinv.reshape(RB, col_blocks, BLOCK, BLOCK).astype(jnp.float32)
    applied = jnp.einsum('rcik,rckj->rcij', linv, blocks_wide).astype(jnp.bfloat16)
    precond = jnp.einsum('rcik,rckj->rcij', applied.astype(jnp.float32), rinv)
    gnorm = lax.optimization_barrier(jnp.sum(blocks_wide * blocks_wide, axis=(2, 3)))
    pnorm = lax.optimization_barrier(jnp.sum(precond * precond, axis=(2, 3)))
    scale = clip_factor * jnp.sqrt(gnorm) / (jnp.sqrt(pnorm) + epsilon)
    update = (scale[:, :, None, None] * precond).astype(jnp.bfloat16)
    update = update.transpose(0, 2, 1, 3).reshape(ROWS, COLS)
    new_momentum = momentum_rate * momentum + update.astype(jnp.float32)
    return (new_momentum, new_left.reshape(RB, 2 * col_blocks, HALF, BLOCK), new_right.reshape(RB, 2 * col_blocks, HALF, BLOCK))
```

```python
import functools
import math

import jax
import jax.numpy as jnp
from jax import lax
from jax.experimental import pallas as pl
from jax.experimental.pallas import tpu as pltpu
from jax.sharding import PartitionSpec as P

decay_stat = 0.95
momentum_rate = 0.9
epsilon = 1e-06
lanes = 128
extra_rows = 8
ring_x = 4
ring_z = 8
pairs = ring_z // 2
origins = (0, -1, -2, -3, 1, 2, 3, 4)


def shifted(block, step_x, step_z):
    route = []
    for x in range(ring_x):
        for z in range(ring_z):
            there = (x + step_x) % ring_x * ring_z + (z + step_z(z)) % ring_z
            route.append((x * ring_z + z, there))
    return lax.ppermute(block, "fsdp", route)


def toward(block, steps):
    return shifted(block, 0, lambda z: steps if z % 2 else -steps)


def scalar_sum(value):
    return jnp.sum(jnp.sum(value, axis=0, keepdims=True), axis=1, keepdims=True)


def aligned(index, multiple):
    return pl.multiple_of(index * multiple, multiple)


def cut_kernel(place, grad, *rest):
    *slabs, sem = rest
    x = place[0] // ring_z
    width = slabs[0].shape[1]
    copies = []
    for i, slab in enumerate(slabs):
        at = pl.ds(aligned((x + 1 + i) % ring_x, width), width)
        copies.append(pltpu.make_async_copy(grad.at[:, at], slab, sem.at[i]))
        copies[-1].start()
    for copy in copies:
        copy.wait()


def pick_kernel(place, *rest):
    slabs, outs = rest[:ring_x], rest[ring_x:]
    z = place[0] % ring_z
    pair, parity = z // 2, z % 2
    width = outs[0].shape[2]
    for out, step in zip(outs, (2, 1 - 2 * parity, 2 * parity - 1, 0)):
        column = (pair + pairs + step) % pairs
        for d in range(ring_x):
            out[d] = slabs[d][:, pl.ds(aligned(column, width), width)]


def apply_kernel(place, *refs):
    groups, (own_root, partner_root, right_root) = refs[:8], refs[8:11]
    blocks, payload, root_v, right_v, sem = refs[11:]
    bring = pltpu.make_async_copy(right_root, right_v, sem)
    bring.start()
    me = place[0]
    x, z = me // ring_z, me % ring_z
    parity = z % 2
    sign = 1 - 2 * parity
    rows_dev = groups[0].shape[1]
    row_blocks, half, block_size = own_root.shape
    owners, length, _ = payload.shape
    body = length - extra_rows

    for group, origin in zip(groups, origins):
        for d in range(ring_x):
            source = (x + ring_x - d) % ring_x * ring_z + (z + ring_z + sign * origin) % ring_z
            blocks[pl.ds(aligned(source, rows_dev), rows_dev), :] = group[d]
    for root, side in ((own_root, parity), (partner_root, 1 - parity)):
        for r in range(row_blocks):
            root_v[r, pl.ds(aligned(side, half), half), :] = root[r]
    bring.wait()

    lane = lax.broadcasted_iota(jnp.int32, (8, lanes), 1)
    total = jnp.zeros((8, lanes), jnp.float32)
    for r in range(row_blocks):
        begin, end = r * block_size, (r + 1) * block_size
        block = blocks[begin:end, :]
        applied = jnp.dot(root_v[r], block, preferred_element_type=jnp.float32)
        precond = jnp.dot(
            applied.astype(jnp.bfloat16), right_v[r], preferred_element_type=jnp.float32
        )
        rounded = precond.astype(jnp.bfloat16)
        for f in range(begin // rows_dev, -(-end // rows_dev)):
            low, high = max(begin, f * rows_dev), min(end, (f + 1) * rows_dev)
            for c in range(half // lanes):
                at = c * rows_dev - f * rows_dev
                payload[f, at + low : at + high, :] = rounded[
                    low - begin : high - begin, c * lanes : (c + 1) * lanes
                ]
        wide = block.astype(jnp.float32)
        total += jnp.where(lane == r, scalar_sum(precond * precond), 0.0)
        total += jnp.where(lane == r + row_blocks, scalar_sum(wide * wide), 0.0)

    high = total.astype(jnp.bfloat16).astype(jnp.float32)
    middle = (total - high).astype(jnp.bfloat16).astype(jnp.float32)
    low = total - high - middle
    row = lax.broadcasted_iota(jnp.int32, (8, lanes), 0)
    parts = jnp.where(row == 0, high, jnp.where(row == 1, middle, jnp.where(row == 2, low, 0.0)))
    parts = parts.astype(jnp.bfloat16)
    for f in range(owners):
        payload[f, body : body + extra_rows, :] = parts


def gram_kernel(
    place, blocks, left_stat, right_stat, momentum,
    left_gram, right_gram, left_near, right_near, momentum_near, sem,
):
    bring = []
    for i, (far, near) in enumerate(
        ((left_stat, left_near), (right_stat, right_near), (momentum, momentum_near))
    ):
        bring.append(pltpu.make_async_copy(far, near, sem.at[i]))
        bring[-1].start()
    row_blocks, half, block_size = left_gram.shape
    parity = place[0] % 2
    for r in range(row_blocks):
        block = blocks[r * block_size : (r + 1) * block_size, :]
        rows = blocks[pl.ds(pl.multiple_of(r * block_size + parity * half, half), half), :]
        left_gram[r] = lax.dot_general(
            rows, block, (((1,), (1,)), ((), ())), preferred_element_type=jnp.float32
        )
    for side in range(2):

        @pl.when(parity == side)
        def _():
            for r in range(row_blocks):
                block = blocks[r * block_size : (r + 1) * block_size, :]
                right_gram[r] = lax.dot_general(
                    block[:, side * half : (side + 1) * half], block,
                    (((0,), (0,)), ((), ())), preferred_element_type=jnp.float32,
                )
    for copy in bring:
        copy.wait()


def finish_kernel(
    clip_limit, block_size, place,
    back, momentum, left_stat, right_stat, left_gram, right_gram,
    new_momentum, new_left, new_right, momentum_v, stat_v, out_sem, stat_out_sem,
):
    me = place[0]
    rows_dev, all_cols = momentum.shape
    owners, length, _ = back.shape
    row_blocks, half, _ = left_stat.shape
    pieces = out_sem.shape[0]
    width = all_cols // pieces
    share = owners // pieces
    columns = all_cols // owners
    body = length - extra_rows

    parts = back[:, body : body + extra_rows, :].astype(jnp.float32)
    values = parts[:, 0, :] + parts[:, 1, :] + parts[:, 2, :]
    lane = lax.broadcasted_iota(jnp.int32, values.shape, 1)
    source = lax.broadcasted_iota(jnp.int32, values.shape, 0)
    even = source % 2 == 0
    paired = jnp.where(even, pltpu.roll(values, owners - 1, 0), pltpu.roll(values, 1, 0))
    pnorm = values + paired
    gnorm = pltpu.roll(values, lanes - row_blocks, 1)
    total_sq = scalar_sum(jnp.where(even & (lane < row_blocks), gnorm, 0.0))
    clip_factor = jnp.minimum(1.0, clip_limit / (jnp.sqrt(total_sq) + epsilon))
    coeff = (1.0 - decay_stat) * clip_factor * clip_factor
    puts = []
    for side, (stat, gram, out) in enumerate(
        ((left_stat, left_gram, new_left), (right_stat, right_gram, new_right))
    ):
        for r in range(row_blocks):
            i = side * row_blocks + r
            stat_v[i] = decay_stat * stat[r] + coeff * gram[r]
            puts.append(pltpu.make_async_copy(stat_v.at[i], out.at[r], stat_out_sem.at[i]))
            puts[-1].start()

    scale = clip_factor * jnp.sqrt(gnorm) / (jnp.sqrt(pnorm) + epsilon)
    first = me * rows_dev // block_size
    until = (first + 1) * block_size - me * rows_dev
    upper = jnp.sum(jnp.where(lane == first, scale, 0.0), axis=1, keepdims=True)
    lower = jnp.sum(
        jnp.where((lane == first + 1) & (lane < row_blocks), scale, 0.0), axis=1, keepdims=True
    )
    in_upper = lax.broadcasted_iota(jnp.int32, (rows_dev, lanes), 0) < until
    for q in range(pieces):
        for s in range(q * share, (q + 1) * share):
            row_scale = jnp.where(in_upper, upper[s : s + 1], lower[s : s + 1])
            for c in range(columns // lanes):
                at = pl.ds(s * columns + c * lanes, lanes)
                moved = back[s, c * rows_dev : (c + 1) * rows_dev, :].astype(jnp.float32)
                momentum_v[:, at] = momentum_rate * momentum[:, at] + row_scale * moved
        part = pl.ds(q * width, width)
        puts.append(
            pltpu.make_async_copy(momentum_v.at[:, part], new_momentum.at[:, part], out_sem.at[q])
        )
        puts[-1].start()
    for copy in puts:
        copy.wait()


def keep_in_hbm(array):
    return pltpu.with_memory_space_constraint(array, pltpu.HBM)


def local(grad, momentum, left_stat, right_stat, left_root, right_root):
    owners = ring_x * ring_z
    me = lax.axis_index("fsdp")
    place = me.astype(jnp.int32).reshape(1)
    rows_dev, all_cols = grad.shape
    row_blocks, _, half, block_size = left_stat.shape
    all_rows = rows_dev * owners
    clip_limit = 0.5 * math.sqrt(all_rows * all_cols)
    length = rows_dev * half // lanes + extra_rows
    slab_width = all_cols // ring_x
    smem = pl.BlockSpec(memory_space=pltpu.SMEM)
    in_hbm = pl.BlockSpec(memory_space=pltpu.HBM)
    in_vmem = pl.BlockSpec(memory_space=pltpu.VMEM)
    some_vmem = pltpu.CompilerParams(vmem_limit_bytes=16 << 20)
    flops = row_blocks * 2 * half * block_size * block_size
    dma = pltpu.SemaphoreType.DMA

    def cost(flops, megabytes):
        return pl.CostEstimate(flops=flops, bytes_accessed=megabytes << 20, transcendentals=0)

    def array(*shape, dtype=jnp.bfloat16):
        return jax.ShapeDtypeStruct(shape, dtype)

    left_root = left_root.reshape(row_blocks, half, block_size)
    right_root = right_root.reshape(row_blocks, block_size, half)
    left_stat = left_stat.reshape(row_blocks, half, block_size)
    right_stat = right_stat.reshape(row_blocks, half, block_size)

    *slabs, own_slab = pl.pallas_call(
        cut_kernel,
        out_shape=[array(rows_dev, slab_width)] * ring_x,
        in_specs=[smem, in_hbm],
        out_specs=[in_vmem] * ring_x,
        scratch_shapes=[dma((ring_x,))],
        cost_estimate=cost(0, 1),
        name="cut",
    )(place, keep_in_hbm(grad))
    slabs = [shifted(slab, d + 1, lambda z: 0) for d, slab in enumerate(slabs)]
    swap = functools.partial(
        lax.ppermute, axis_name="fsdp", perm=[(i, i ^ 1) for i in range(owners)]
    )
    left_partner = swap(left_root)
    far, same, cross, own = pl.pallas_call(
        pick_kernel,
        out_shape=[array(ring_x, rows_dev, block_size)] * 4,
        in_specs=[smem] + [in_vmem] * ring_x,
        out_specs=[in_vmem] * 4,
        cost_estimate=cost(0, 2),
        name="pick",
    )(place, own_slab, *slabs)
    far = toward(far, 3)
    same = toward(same, -2)
    cross = toward(cross, 1)
    groups = [own, cross, same, far]
    groups += [swap(group) for group in groups]

    blocks, payload = pl.pallas_call(
        apply_kernel,
        out_shape=[array(all_rows, block_size), array(owners, length, lanes)],
        in_specs=[smem] + [in_vmem] * 10 + [in_hbm],
        out_specs=[in_vmem] * 2,
        scratch_shapes=[
            pltpu.VMEM((row_blocks, block_size, block_size), jnp.bfloat16),
            pltpu.VMEM((row_blocks, block_size, half), jnp.bfloat16),
            dma,
        ],
        compiler_params=some_vmem,
        cost_estimate=cost(3 * flops, 6),
        name="apply",
    )(place, *groups, left_root, left_partner, keep_in_hbm(right_root))
    back = lax.all_to_all(payload, "fsdp", split_axis=0, concat_axis=0, tiled=True)

    stat = array(row_blocks, half, block_size, dtype=jnp.float32)
    wide = array(rows_dev, all_cols, dtype=jnp.float32)
    grams = pl.pallas_call(
        gram_kernel,
        out_shape=[stat] * 4 + [wide],
        in_specs=[smem, in_vmem] + [in_hbm] * 3,
        out_specs=[in_vmem] * 5,
        scratch_shapes=[dma((3,))],
        compiler_params=some_vmem,
        cost_estimate=cost(2 * flops, 8),
        name="grams",
    )(place, blocks, *map(keep_in_hbm, (left_stat, right_stat, momentum)))
    left_gram, right_gram, left_near, right_near, momentum_near = grams

    quarters = 4
    new_momentum, new_left, new_right = pl.pallas_call(
        functools.partial(finish_kernel, clip_limit, block_size),
        out_shape=[wide, stat, stat],
        in_specs=[smem] + [in_vmem] * 6,
        out_specs=[in_hbm] * 3,
        scratch_shapes=[
            pltpu.VMEM((rows_dev, all_cols), jnp.float32),
            pltpu.VMEM((2 * row_blocks, half, block_size), jnp.float32),
            dma((quarters,)),
            dma((2 * row_blocks,)),
        ],
        compiler_params=some_vmem,
        cost_estimate=cost(1 << 22, 10),
        name="finish",
    )(place, back, momentum_near, left_near, right_near, left_gram, right_gram)
    shape = (row_blocks, 1, half, block_size)
    return (new_momentum, new_left.reshape(shape), new_right.reshape(shape))


def solution(mesh):
    return jax.shard_map(
        local,
        mesh=mesh,
        in_specs=(
            P(("section", "fsdp"), None),
            P(("section", "fsdp"), None),
            P("section", "fsdp", None, None),
            P("section", "fsdp", None, None),
            P("section", "fsdp", None, None),
            P("section", "fsdp", None, None),
        ),
        out_specs=(
            P(("section", "fsdp"), None),
            P("section", "fsdp", None, None),
            P("section", "fsdp", None, None),
        ),
        check_vma=False,
    )
```

```python
import functools
import math

import jax
import jax.numpy as jnp
from jax import lax
from jax.experimental import pallas as pl
from jax.experimental.pallas import tpu as pltpu
from jax.sharding import PartitionSpec as P

decay_stat = 0.95
momentum_rate = 0.9
epsilon = 1e-06
lanes = 128
extra_rows = 8
row_parts = 3
ring_x = 4
ring_z = 8
pairs = ring_z // 2
origins = (-3, -2, -1, 0, 4, 3, 2, 1)


def shifted(block, step_x, step_z):
    route = []
    for x in range(ring_x):
        for z in range(ring_z):
            there = (x + step_x) % ring_x * ring_z + (z + step_z(z)) % ring_z
            route.append((x * ring_z + z, there))
    return lax.ppermute(block, "fsdp", route)


def toward(block, steps):
    return shifted(block, 0, lambda z: steps if z % 2 else -steps)


def scalar_sum(value):
    return jnp.sum(jnp.sum(value, axis=0, keepdims=True), axis=1, keepdims=True)


def aligned(index, multiple):
    return pl.multiple_of(index * multiple, multiple)


def role_steps(parity):
    return 2, 1 - 2 * parity, 2 * parity - 1, 0


def cut_kernel(place, grad, slabs, *rest):
    nears, sem = rest[:-1], rest[-1]
    x, z = place[0] // ring_z, place[0] % ring_z
    pair, parity = z // 2, z % 2
    _, rows_dev, width = slabs.shape
    block_size = nears[0].shape[1]
    wanted = [(slabs.at[i], pl.ds(i * width, width)) for i in range(ring_x)]
    for near, step in zip(nears, role_steps(parity)):
        at = x * pairs + (pair + pairs + step) % pairs
        wanted.append((near, pl.ds(aligned(at, block_size), block_size)))
    copies = []
    for out, at in wanted:
        for part in range(row_parts):
            rows = pl.ds(part * rows_dev // row_parts, rows_dev // row_parts)
            copies.append(
                pltpu.make_async_copy(grad.at[rows, at], out.at[rows], sem.at[len(copies)])
            )
            copies[-1].start()
    for copy in copies:
        copy.wait()


def pick_kernel(place, slabs, *rest):
    outs, sem = rest[:-1], rest[-1]
    x, z = place[0] // ring_z, place[0] % ring_z
    pair, parity = z // 2, z % 2
    width = outs[0].shape[2]
    copies = []
    for out, step in zip(outs, role_steps(parity)):
        at = pl.ds(aligned((pair + pairs + step) % pairs, width), width)
        for d in range(1, ring_x):
            block = slabs.at[(x + ring_x - d) % ring_x, :, at]
            copies.append(pltpu.make_async_copy(block, out.at[d - 1], sem.at[len(copies)]))
            copies[-1].start()
    for copy in copies:
        copy.wait()


def apply_kernel(place, *refs):
    nears, swapped, fars = refs[:4], refs[4], refs[5:13]
    own_root, partner_root, right_root, blocks, payload, root_v, right_v, sem = refs[13:]
    me = place[0]
    x, z = me // ring_z, me % ring_z
    parity = z % 2
    sign = 1 - 2 * parity
    rows_dev = nears[0].shape[0]
    row_blocks, half, block_size = own_root.shape
    owners, length, _ = payload.shape
    body = length - extra_rows

    bring = [pltpu.make_async_copy(right_root, right_v, sem.at[2])]
    for i, (root, side) in enumerate(((own_root, parity), (partner_root, 1 - parity))):
        rows = pl.ds(aligned(side, half), half)
        bring.append(pltpu.make_async_copy(root, root_v.at[:, rows], sem.at[i]))
    for copy in bring[::-1]:
        copy.start()
    for i, origin in enumerate(origins):
        for d in range(ring_x):
            source = (x + ring_x - d) % ring_x * ring_z + (z + ring_z + sign * origin) % ring_z
            group = fars[i][d - 1] if d else nears[i][...] if i < 4 else swapped[i - 4]
            blocks[pl.ds(aligned(source, rows_dev), rows_dev), :] = group
    for copy in bring:
        copy.wait()

    lane = lax.broadcasted_iota(jnp.int32, (8, lanes), 1)
    total = jnp.zeros((8, lanes), jnp.float32)
    for r in range(row_blocks):
        begin, end = r * block_size, (r + 1) * block_size
        block = blocks[begin:end, :]
        applied = jnp.dot(root_v[r], block, preferred_element_type=jnp.float32)
        precond = jnp.dot(
            applied.astype(jnp.bfloat16), right_v[r], preferred_element_type=jnp.float32
        )
        rounded = precond.astype(jnp.bfloat16)
        for f in range(begin // rows_dev, -(-end // rows_dev)):
            low, high = max(begin, f * rows_dev), min(end, (f + 1) * rows_dev)
            for c in range(half // lanes):
                at = c * rows_dev - f * rows_dev
                payload[f, at + low : at + high, :] = rounded[
                    low - begin : high - begin, c * lanes : (c + 1) * lanes
                ]
        wide = block.astype(jnp.float32)
        total += jnp.where(lane == r, scalar_sum(precond * precond), 0.0)
        total += jnp.where(lane == r + row_blocks, scalar_sum(wide * wide), 0.0)

    high = total.astype(jnp.bfloat16).astype(jnp.float32)
    middle = (total - high).astype(jnp.bfloat16).astype(jnp.float32)
    low = total - high - middle
    row = lax.broadcasted_iota(jnp.int32, (8, lanes), 0)
    parts = jnp.where(row == 0, high, jnp.where(row == 1, middle, jnp.where(row == 2, low, 0.0)))
    parts = parts.astype(jnp.bfloat16)
    for f in range(owners):
        payload[f, body : body + extra_rows, :] = parts


def gram_kernel(place, blocks, left_gram, right_gram):
    row_blocks, half, block_size = left_gram.shape
    parity = place[0] % 2
    for r in range(row_blocks):
        block = blocks[r * block_size : (r + 1) * block_size, :]
        rows = blocks[pl.ds(pl.multiple_of(r * block_size + parity * half, half), half), :]
        left_gram[r] = lax.dot_general(
            rows, block, (((1,), (1,)), ((), ())), preferred_element_type=jnp.float32
        )
    for side in range(2):

        @pl.when(parity == side)
        def _():
            for r in range(row_blocks):
                block = blocks[r * block_size : (r + 1) * block_size, :]
                right_gram[r] = lax.dot_general(
                    block[:, side * half : (side + 1) * half], block,
                    (((0,), (0,)), ((), ())), preferred_element_type=jnp.float32,
                )


def finish_kernel(
    clip_limit, block_size, place,
    back, momentum, left_stat, right_stat, left_gram, right_gram,
    new_momentum, new_left, new_right,
    back_v, momentum_v, stat_v, gram_v, back_sem, in_sem, stat_sem, gram_sem, out_sem, stat_out_sem,
):
    me = place[0]
    rows_dev, all_cols = momentum.shape
    owners, length, _ = back.shape
    row_blocks, half, _ = left_stat.shape
    pieces = out_sem.shape[0]
    width = all_cols // pieces
    share = owners // pieces
    columns = all_cols // owners
    body = length - extra_rows

    get_back, get_momentum, put_momentum = [], [], []
    get_stat, get_gram, put_stat = [], [], []
    for q in range(pieces):
        some = pl.ds(q * share, share)
        get_back.append(pltpu.make_async_copy(back.at[some], back_v.at[some], back_sem.at[q]))
        get_back[-1].start()
    for side, (stat, gram, out) in enumerate(
        ((left_stat, left_gram, new_left), (right_stat, right_gram, new_right))
    ):
        for r in range(row_blocks):
            i = side * row_blocks + r
            get_stat.append(pltpu.make_async_copy(stat.at[r], stat_v.at[i], stat_sem.at[i]))
            get_gram.append(pltpu.make_async_copy(gram.at[r], gram_v.at[i], gram_sem.at[i]))
            put_stat.append(pltpu.make_async_copy(stat_v.at[i], out.at[r], stat_out_sem.at[i]))
            get_stat[-1].start()
            get_gram[-1].start()
    for q in range(pieces):
        part = pl.ds(q * width, width)
        get_momentum.append(
            pltpu.make_async_copy(momentum.at[:, part], momentum_v.at[:, part], in_sem.at[q])
        )
        put_momentum.append(
            pltpu.make_async_copy(momentum_v.at[:, part], new_momentum.at[:, part], out_sem.at[q])
        )
        get_momentum[-1].start()

    for copy in get_back:
        copy.wait()
    parts = back_v[:, body : body + extra_rows, :].astype(jnp.float32)
    values = parts[:, 0, :] + parts[:, 1, :] + parts[:, 2, :]
    lane = lax.broadcasted_iota(jnp.int32, values.shape, 1)
    source = lax.broadcasted_iota(jnp.int32, values.shape, 0)
    even = source % 2 == 0
    paired = jnp.where(even, pltpu.roll(values, owners - 1, 0), pltpu.roll(values, 1, 0))
    pnorm = values + paired
    gnorm = pltpu.roll(values, lanes - row_blocks, 1)
    total_sq = scalar_sum(jnp.where(even & (lane < row_blocks), gnorm, 0.0))
    clip_factor = jnp.minimum(1.0, clip_limit / (jnp.sqrt(total_sq) + epsilon))
    coeff = (1.0 - decay_stat) * clip_factor * clip_factor
    for i in range(2 * row_blocks):
        get_stat[i].wait()
        get_gram[i].wait()
        stat_v[i] = decay_stat * stat_v[i] + coeff * gram_v[i]
        put_stat[i].start()

    scale = clip_factor * jnp.sqrt(gnorm) / (jnp.sqrt(pnorm) + epsilon)
    first = me * rows_dev // block_size
    until = (first + 1) * block_size - me * rows_dev
    upper = jnp.sum(jnp.where(lane == first, scale, 0.0), axis=1, keepdims=True)
    lower = jnp.sum(
        jnp.where((lane == first + 1) & (lane < row_blocks), scale, 0.0), axis=1, keepdims=True
    )
    in_upper = lax.broadcasted_iota(jnp.int32, (rows_dev, lanes), 0) < until
    for q in range(pieces):
        get_momentum[q].wait()
        for s in range(q * share, (q + 1) * share):
            row_scale = jnp.where(in_upper, upper[s : s + 1], lower[s : s + 1])
            for c in range(columns // lanes):
                at = pl.ds(s * columns + c * lanes, lanes)
                moved = back_v[s, c * rows_dev : (c + 1) * rows_dev, :].astype(jnp.float32)
                momentum_v[:, at] = momentum_rate * momentum_v[:, at] + row_scale * moved
        put_momentum[q].start()
    for copy in put_stat + put_momentum:
        copy.wait()


def keep_in_hbm(array):
    return pltpu.with_memory_space_constraint(array, pltpu.HBM)


def local(grad, momentum, left_stat, right_stat, left_root, right_root):
    owners = ring_x * ring_z
    me = lax.axis_index("fsdp")
    place = me.astype(jnp.int32).reshape(1)
    rows_dev, all_cols = grad.shape
    row_blocks, _, half, block_size = left_stat.shape
    all_rows = rows_dev * owners
    clip_limit = 0.5 * math.sqrt(all_rows * all_cols)
    length = rows_dev * half // lanes + extra_rows
    slab_width = all_cols // ring_x
    smem = pl.BlockSpec(memory_space=pltpu.SMEM)
    in_hbm = pl.BlockSpec(memory_space=pltpu.HBM)
    in_vmem = pl.BlockSpec(memory_space=pltpu.VMEM)
    some_vmem = pltpu.CompilerParams(vmem_limit_bytes=16 << 20)
    flops = row_blocks * 2 * half * block_size * block_size
    dma = pltpu.SemaphoreType.DMA

    def cost(flops, megabytes):
        return pl.CostEstimate(flops=flops, bytes_accessed=megabytes << 20, transcendentals=0)

    def array(*shape, dtype=jnp.bfloat16):
        return jax.ShapeDtypeStruct(shape, dtype)

    left_root = left_root.reshape(row_blocks, half, block_size)
    right_root = right_root.reshape(row_blocks, block_size, half)
    left_stat = left_stat.reshape(row_blocks, half, block_size)
    right_stat = right_stat.reshape(row_blocks, half, block_size)

    slabs, *nears = pl.pallas_call(
        cut_kernel,
        out_shape=[array(ring_x, rows_dev, slab_width)] + [array(rows_dev, block_size)] * 4,
        in_specs=[smem, in_hbm],
        out_specs=[in_vmem] * 5,
        scratch_shapes=[dma(((ring_x + 4) * row_parts,))],
        cost_estimate=cost(0, 1),
        name="cut",
    )(place, keep_in_hbm(grad))
    slabs = lax.all_to_all(
        slabs, "fsdp", split_axis=0, concat_axis=0, tiled=True,
        axis_index_groups=[[i * ring_z + z for i in range(ring_x)] for z in range(ring_z)],
    )
    steps = (3, -2, 1)
    nears = [toward(near, step) for near, step in zip(nears, steps)] + nears[3:]
    swap = functools.partial(
        lax.ppermute, axis_name="fsdp", perm=[(i, i ^ 1) for i in range(owners)]
    )
    left_partner = swap(left_root)
    fars = pl.pallas_call(
        pick_kernel,
        out_shape=[array(ring_x - 1, rows_dev, block_size)] * 4,
        in_specs=[smem, in_hbm],
        out_specs=[in_vmem] * 4,
        scratch_shapes=[dma((4 * (ring_x - 1),))],
        cost_estimate=cost(0, 2),
        name="pick",
    )(place, slabs)
    fars = [toward(far, step) for far, step in zip(fars, steps)] + [fars[3]]
    swapped = swap(jnp.stack(nears))
    fars += [swap(far) for far in fars]

    blocks, payload = pl.pallas_call(
        apply_kernel,
        out_shape=[array(all_rows, block_size), array(owners, length, lanes)],
        in_specs=[smem] + [in_vmem] * 13 + [in_hbm] * 3,
        out_specs=[in_vmem] * 2,
        scratch_shapes=[
            pltpu.VMEM((row_blocks, block_size, block_size), jnp.bfloat16),
            pltpu.VMEM((row_blocks, block_size, half), jnp.bfloat16),
            dma((3,)),
        ],
        compiler_params=some_vmem,
        cost_estimate=cost(3 * flops, 6),
        name="apply",
    )(place, *nears, swapped, *fars, keep_in_hbm(left_root), left_partner, keep_in_hbm(right_root))
    back = lax.all_to_all(payload, "fsdp", split_axis=0, concat_axis=0, tiled=True)

    stat = array(row_blocks, half, block_size, dtype=jnp.float32)
    wide = array(rows_dev, all_cols, dtype=jnp.float32)
    grams = pl.pallas_call(
        gram_kernel,
        out_shape=[stat] * 2,
        in_specs=[smem, in_vmem],
        out_specs=[in_vmem] * 2,
        compiler_params=some_vmem,
        cost_estimate=cost(2 * flops, 5),
        name="grams",
    )(place, blocks)

    quarters = 4
    new_momentum, new_left, new_right = pl.pallas_call(
        functools.partial(finish_kernel, clip_limit, block_size),
        out_shape=[wide, stat, stat],
        in_specs=[smem] + [in_hbm] * 6,
        out_specs=[in_hbm] * 3,
        scratch_shapes=[
            pltpu.VMEM((owners, length, lanes), jnp.bfloat16),
            pltpu.VMEM((rows_dev, all_cols), jnp.float32),
            pltpu.VMEM((2 * row_blocks, half, block_size), jnp.float32),
            pltpu.VMEM((2 * row_blocks, half, block_size), jnp.float32),
            dma((quarters,)),
            dma((quarters,)),
            dma((2 * row_blocks,)),
            dma((2 * row_blocks,)),
            dma((quarters,)),
            dma((2 * row_blocks,)),
        ],
        compiler_params=some_vmem,
        cost_estimate=cost(1 << 22, 14),
        name="finish",
    )(place, back, *map(keep_in_hbm, (momentum, left_stat, right_stat, *grams)))
    shape = (row_blocks, 1, half, block_size)
    return (new_momentum, new_left.reshape(shape), new_right.reshape(shape))


def solution(mesh):
    return jax.shard_map(
        local,
        mesh=mesh,
        in_specs=(
            P(("section", "fsdp"), None),
            P(("section", "fsdp"), None),
            P("section", "fsdp", None, None),
            P("section", "fsdp", None, None),
            P("section", "fsdp", None, None),
            P("section", "fsdp", None, None),
        ),
        out_specs=(
            P(("section", "fsdp"), None),
            P("section", "fsdp", None, None),
            P("section", "fsdp", None, None),
        ),
        check_vma=False,
    )
```

```python
import functools
import math

import jax
import jax.numpy as jnp
from jax import lax
from jax.experimental import pallas as pl
from jax.experimental.pallas import tpu as pltpu
from jax.sharding import PartitionSpec as P

decay_stat = 0.95
momentum_rate = 0.9
epsilon = 1e-06
lanes = 128
extra_rows = 8
ring_x = 4
ring_z = 8
pairs = ring_z // 2
roles = 4
origins = (-3, -2, -1, 0, 4, 3, 2, 1)


def shifted(block, step_x, step_z):
    route = []
    for x in range(ring_x):
        for z in range(ring_z):
            there = (x + step_x) % ring_x * ring_z + (z + step_z(z)) % ring_z
            route.append((x * ring_z + z, there))
    return lax.ppermute(block, "fsdp", route)


def outward(steps):
    return lambda z: steps if z % 2 else -steps


def scalar_sum(value):
    return jnp.sum(jnp.sum(value, axis=0, keepdims=True), axis=1, keepdims=True)


def aligned(index, multiple):
    return pl.multiple_of(index * multiple, multiple)


def in_parts(value):
    value = jnp.broadcast_to(value, (extra_rows, value.shape[1]))
    high = value.astype(jnp.bfloat16).astype(jnp.float32)
    middle = (value - high).astype(jnp.bfloat16).astype(jnp.float32)
    low = value - high - middle
    row = lax.broadcasted_iota(jnp.int32, value.shape, 0)
    parts = jnp.where(row == 0, high, jnp.where(row == 1, middle, jnp.where(row == 2, low, 0.0)))
    return parts.astype(jnp.bfloat16)


def from_parts(rows):
    wide = rows.astype(jnp.float32)
    return jnp.sum(wide, axis=0, keepdims=True)


def cut_kernel(place, grad, *rest):
    outs, sem = rest[:-1], rest[-1]
    pair, parity = place[0] % ring_z // 2, place[0] % 2
    rows_dev = grad.shape[0]
    width = outs[0].shape[1]
    body = ring_x * rows_dev
    copies = []
    for out, step in zip(outs, (2, 1 - 2 * parity, 2 * parity - 1, 0)):
        column = (pair + pairs + step) % pairs
        for x in range(ring_x):
            at = pl.ds(aligned(x * pairs + column, width), width)
            rows = pl.ds(x * rows_dev, rows_dev)
            copies.append(pltpu.make_async_copy(grad.at[:, at], out.at[rows], sem.at[len(copies)]))
            copies[-1].start()
    square = jnp.zeros((8, width), jnp.float32)
    for i, copy in enumerate(copies):
        copy.wait()
        first = i % ring_x * rows_dev
        for row in range(first, first + rows_dev, 16):
            wide = outs[i // ring_x][row : row + 16, :].astype(jnp.float32)
            square += wide[:8] * wide[:8] + wide[8:] * wide[8:]
    parts = in_parts(jnp.broadcast_to(scalar_sum(square), (1, width)))
    for out in outs:
        out[body : body + extra_rows, :] = parts


def hold_kernel(root, earlier, out, sem):
    last = out.shape[0]
    copy = pltpu.make_async_copy(root.at[pl.ds(root.shape[0] - last, last)], out, sem)
    copy.start()
    copy.wait()


def pick_kernel(place, *refs):
    groups, outs = refs[:roles], refs[roles:]
    x = place[0] // ring_z
    body = groups[0].shape[0] - extra_rows
    rows_dev = body // ring_x
    total = sum(from_parts(group[body : body + extra_rows, :]) for group in groups)
    parts = in_parts(total)
    for d, out in enumerate(outs):
        rows = pl.ds(aligned((x + d) % ring_x, rows_dev), rows_dev)
        for i, group in enumerate(groups):
            out[i * rows_dev : (i + 1) * rows_dev, :] = group[rows, :]
        out[body : body + extra_rows, :] = parts


def apply_kernel(clip_limit, place, *refs):
    groups = refs[: 2 * ring_x]
    own_root, partner_first, partner_last, right_root = refs[8:12]
    blocks, payload, clip, root_v, right_v, sem = refs[12:]
    me = place[0]
    x, z = me // ring_z, me % ring_z
    parity = z % 2
    sign = 1 - 2 * parity
    row_blocks, half, block_size = own_root.shape
    owners, length, _ = payload.shape
    body = length - extra_rows
    group_body = groups[0].shape[0] - extra_rows
    rows_dev = group_body // roles

    own_rows, partner_rows = (pl.ds(aligned(side, half), half) for side in (parity, 1 - parity))
    early = partner_first.shape[0]
    first, last = pl.ds(0, early), pl.ds(early, row_blocks - early)
    bring = [
        pltpu.make_async_copy(own_root, root_v.at[:, own_rows], sem.at[0]),
        pltpu.make_async_copy(partner_first, root_v.at[first, partner_rows], sem.at[1]),
        pltpu.make_async_copy(partner_last, root_v.at[last, partner_rows], sem.at[3]),
        pltpu.make_async_copy(right_root, right_v, sem.at[2]),
    ]
    for copy in bring:
        copy.start()
    for i, origin in enumerate(origins):
        for d in range(ring_x):
            source = (x + ring_x - d) % ring_x * ring_z + (z + ring_z + sign * origin) % ring_z
            group = groups[i // roles * ring_x + d]
            first = i % roles * rows_dev
            blocks[pl.ds(aligned(source, rows_dev), rows_dev), :] = group[first : first + rows_dev, :]
    total_sq = sum(from_parts(group[group_body : group_body + extra_rows, :]) for group in groups)
    clip_factor = jnp.minimum(1.0, clip_limit / (jnp.sqrt(total_sq) + epsilon))
    clip[...] = jnp.broadcast_to(clip_factor[:, :lanes], clip.shape)
    for copy in bring:
        copy.wait()

    lane = lax.broadcasted_iota(jnp.int32, (1, lanes), 1)
    total = jnp.zeros((1, lanes), jnp.float32)
    for r in range(row_blocks):
        begin, end = r * block_size, (r + 1) * block_size
        block = blocks[begin:end, :]
        applied = jnp.dot(root_v[r], block, preferred_element_type=jnp.float32)
        precond = jnp.dot(
            applied.astype(jnp.bfloat16), right_v[r], preferred_element_type=jnp.float32
        )
        rounded = precond.astype(jnp.bfloat16)
        for f in range(begin // rows_dev, -(-end // rows_dev)):
            low, high = max(begin, f * rows_dev), min(end, (f + 1) * rows_dev)
            for c in range(half // lanes):
                at = c * rows_dev - f * rows_dev
                payload[f, at + low : at + high, :] = rounded[
                    low - begin : high - begin, c * lanes : (c + 1) * lanes
                ]
        wide = block.astype(jnp.float32)
        total += jnp.where(lane == r, scalar_sum(precond * precond), 0.0)
        total += jnp.where(lane == r + row_blocks, scalar_sum(wide * wide), 0.0)
    parts = in_parts(total)
    for f in range(owners):
        payload[f, body : body + extra_rows, :] = parts


def stat_kernel(
    place, clip, blocks, left_stat, right_stat, new_left, new_right, clip_out, stat_v, in_sem, out_sem
):
    row_blocks, half, block_size = left_stat.shape
    parity = place[0] % 2
    get, put = [], []
    for side, (stat, out) in enumerate(((left_stat, new_left), (right_stat, new_right))):
        for r in range(row_blocks):
            i = side * row_blocks + r
            get.append(pltpu.make_async_copy(stat.at[r], stat_v.at[i], in_sem.at[i]))
            put.append(pltpu.make_async_copy(stat_v.at[i], out.at[r], out_sem.at[i]))
            get[-1].start()
    clip_out[...] = clip[...]
    factor = clip[0:1, 0:1]
    coeff = (1.0 - decay_stat) * factor * factor
    for r in range(row_blocks):
        begin = r * block_size
        block = blocks[begin : begin + block_size, :]
        rows = blocks[pl.ds(pl.multiple_of(begin + parity * half, half), half), :]
        gram = lax.dot_general(
            rows, block, (((1,), (1,)), ((), ())), preferred_element_type=jnp.float32
        )
        get[r].wait()
        stat_v[r] = decay_stat * stat_v[r] + coeff * gram
        put[r].start()
    for r in range(row_blocks):
        i = row_blocks + r
        get[i].wait()
        for side in range(2):

            @pl.when(parity == side)
            def _():
                block = blocks[r * block_size : (r + 1) * block_size, :]
                gram = lax.dot_general(
                    block[:, side * half : (side + 1) * half], block,
                    (((0,), (0,)), ((), ())), preferred_element_type=jnp.float32,
                )
                stat_v[i] = decay_stat * stat_v[i] + coeff * gram

        put[i].start()
    for copy in put:
        copy.wait()


def finish_kernel(
    row_blocks, block_size, place, back, clip, momentum, new_momentum,
    back_v, clip_v, momentum_v, back_sem, clip_sem, in_sem, out_sem,
):
    me = place[0]
    rows_dev, all_cols = momentum.shape
    owners, length, _ = back.shape
    pieces = out_sem.shape[0]
    width = all_cols // pieces
    share = owners // pieces
    columns = all_cols // owners
    body = length - extra_rows

    get_clip = pltpu.make_async_copy(clip, clip_v, clip_sem)
    get_clip.start()
    get_back, get_momentum, put_momentum = [], [], []
    for q in range(pieces):
        some = pl.ds(q * share, share)
        get_back.append(pltpu.make_async_copy(back.at[some], back_v.at[some], back_sem.at[q]))
        get_back[-1].start()
    for q in range(pieces):
        part = pl.ds(q * width, width)
        get_momentum.append(
            pltpu.make_async_copy(momentum.at[:, part], momentum_v.at[:, part], in_sem.at[q])
        )
        put_momentum.append(
            pltpu.make_async_copy(momentum_v.at[:, part], new_momentum.at[:, part], out_sem.at[q])
        )
        get_momentum[-1].start()
    for copy in [get_clip] + get_back:
        copy.wait()

    parts = back_v[:, body : body + extra_rows, :].astype(jnp.float32)
    values = parts[:, 0, :] + parts[:, 1, :] + parts[:, 2, :]
    lane = lax.broadcasted_iota(jnp.int32, values.shape, 1)
    source = lax.broadcasted_iota(jnp.int32, values.shape, 0)
    paired = jnp.where(
        source % 2 == 0, pltpu.roll(values, owners - 1, 0), pltpu.roll(values, 1, 0)
    )
    pnorm = values + paired
    gnorm = pltpu.roll(values, lanes - row_blocks, 1)
    scale = clip_v[0:1, :] * jnp.sqrt(gnorm) / (jnp.sqrt(pnorm) + epsilon)
    first = me * rows_dev // block_size
    until = (first + 1) * block_size - me * rows_dev
    upper = jnp.sum(jnp.where(lane == first, scale, 0.0), axis=1, keepdims=True)
    lower = jnp.sum(
        jnp.where((lane == first + 1) & (lane < row_blocks), scale, 0.0), axis=1, keepdims=True
    )
    in_upper = lax.broadcasted_iota(jnp.int32, (rows_dev, lanes), 0) < until
    for q in range(pieces):
        get_momentum[q].wait()
        for s in range(q * share, (q + 1) * share):
            row_scale = jnp.where(in_upper, upper[s : s + 1], lower[s : s + 1])
            for c in range(columns // lanes):
                at = pl.ds(s * columns + c * lanes, lanes)
                moved = back_v[s, c * rows_dev : (c + 1) * rows_dev, :].astype(jnp.float32)
                momentum_v[:, at] = momentum_rate * momentum_v[:, at] + row_scale * moved
        put_momentum[q].start()
    for copy in put_momentum:
        copy.wait()


def keep_in_hbm(array):
    return pltpu.with_memory_space_constraint(array, pltpu.HBM)


def local(grad, momentum, left_stat, right_stat, left_root, right_root):
    owners = ring_x * ring_z
    place = lax.axis_index("fsdp").astype(jnp.int32).reshape(1)
    rows_dev, all_cols = grad.shape
    row_blocks, _, half, block_size = left_stat.shape
    all_rows = rows_dev * owners
    clip_limit = 0.5 * math.sqrt(all_rows * all_cols)
    length = rows_dev * half // lanes + extra_rows
    smem = pl.BlockSpec(memory_space=pltpu.SMEM)
    in_hbm = pl.BlockSpec(memory_space=pltpu.HBM)
    in_vmem = pl.BlockSpec(memory_space=pltpu.VMEM)
    some_vmem = pltpu.CompilerParams(vmem_limit_bytes=16 << 20)
    flops = row_blocks * 2 * half * block_size * block_size
    dma = pltpu.SemaphoreType.DMA

    def cost(flops, megabytes):
        return pl.CostEstimate(flops=flops, bytes_accessed=megabytes << 20, transcendentals=0)

    def array(*shape, dtype=jnp.bfloat16):
        return jax.ShapeDtypeStruct(shape, dtype)

    left_root = left_root.reshape(row_blocks, half, block_size)
    right_root = right_root.reshape(row_blocks, block_size, half)
    left_stat = left_stat.reshape(row_blocks, half, block_size)
    right_stat = right_stat.reshape(row_blocks, half, block_size)
    group = array(ring_x * rows_dev + extra_rows, block_size)
    stat = array(row_blocks, half, block_size, dtype=jnp.float32)
    wide = array(rows_dev, all_cols, dtype=jnp.float32)
    still = lambda z: 0
    to_partner = outward(-1)

    early = row_blocks - 1
    partner_first = shifted(left_root[:early], 0, to_partner)
    *sent, own = pl.pallas_call(
        cut_kernel,
        out_shape=[group] * roles,
        in_specs=[smem, in_hbm],
        out_specs=[in_vmem] * roles,
        scratch_shapes=[dma((roles * ring_x,))],
        compiler_params=some_vmem,
        cost_estimate=cost(0, 1),
        name="cut",
    )(place, keep_in_hbm(grad))
    far, same, cross = (shifted(block, 0, outward(n)) for block, n in zip(sent, (3, -2, 1)))
    last_root = pl.pallas_call(
        hold_kernel,
        out_shape=array(row_blocks - early, half, block_size),
        in_specs=[in_hbm, in_hbm],
        out_specs=in_vmem,
        scratch_shapes=[dma],
        cost_estimate=cost(0, 1),
        name="hold",
    )(keep_in_hbm(left_root), cross)
    partner_last = shifted(last_root, 0, to_partner)
    parts = pl.pallas_call(
        pick_kernel,
        out_shape=[group] * ring_x,
        in_specs=[smem] + [in_vmem] * roles,
        out_specs=[in_vmem] * ring_x,
        compiler_params=some_vmem,
        cost_estimate=cost(0, 2),
        name="pick",
    )(place, far, same, cross, own)
    near = [parts[0]] + [shifted(parts[d], d, still) for d in range(1, ring_x)]
    swapped = [shifted(parts[d], d, to_partner) for d in range(ring_x) if d != 2]
    swapped.insert(2, shifted(near[2], 0, to_partner))

    blocks, payload, clip = pl.pallas_call(
        functools.partial(apply_kernel, clip_limit),
        out_shape=[
            array(all_rows, block_size),
            array(owners, length, lanes),
            array(8, lanes, dtype=jnp.float32),
        ],
        in_specs=[smem] + [in_vmem] * (2 * ring_x) + [in_hbm] * 4,
        out_specs=[in_vmem] * 3,
        scratch_shapes=[
            pltpu.VMEM((row_blocks, block_size, block_size), jnp.bfloat16),
            pltpu.VMEM((row_blocks, block_size, half), jnp.bfloat16),
            dma((4,)),
        ],
        compiler_params=some_vmem,
        cost_estimate=cost(3 * flops, 6),
        name="apply",
    )(
        place, *near, *swapped,
        keep_in_hbm(left_root), partner_first, partner_last, keep_in_hbm(right_root),
    )
    back = lax.all_to_all(payload, "fsdp", split_axis=0, concat_axis=0, tiled=True)
    new_left, new_right, clip = pl.pallas_call(
        stat_kernel,
        out_shape=[stat] * 2 + [array(8, lanes, dtype=jnp.float32)],
        in_specs=[smem, in_vmem, in_vmem, in_hbm, in_hbm],
        out_specs=[in_hbm, in_hbm, in_vmem],
        scratch_shapes=[
            pltpu.VMEM((2 * row_blocks, half, block_size), jnp.float32),
            dma((2 * row_blocks,)),
            dma((2 * row_blocks,)),
        ],
        compiler_params=some_vmem,
        cost_estimate=cost(2 * flops, 8),
        name="statistics",
    )(place, clip, blocks, keep_in_hbm(left_stat), keep_in_hbm(right_stat))

    quarters = 4
    new_momentum = pl.pallas_call(
        functools.partial(finish_kernel, row_blocks, block_size),
        out_shape=wide,
        in_specs=[smem] + [in_hbm] * 3,
        out_specs=in_hbm,
        scratch_shapes=[
            pltpu.VMEM((owners, length, lanes), jnp.bfloat16),
            pltpu.VMEM((8, lanes), jnp.float32),
            pltpu.VMEM((rows_dev, all_cols), jnp.float32),
            dma((quarters,)),
            dma,
            dma((quarters,)),
            dma((quarters,)),
        ],
        compiler_params=some_vmem,
        cost_estimate=cost(1 << 22, 4),
        name="finish",
    )(place, back, clip, keep_in_hbm(momentum))
    shape = (row_blocks, 1, half, block_size)
    return (new_momentum, new_left.reshape(shape), new_right.reshape(shape))


def solution(mesh):
    return jax.shard_map(
        local,
        mesh=mesh,
        in_specs=(
            P(("section", "fsdp"), None),
            P(("section", "fsdp"), None),
            P("section", "fsdp", None, None),
            P("section", "fsdp", None, None),
            P("section", "fsdp", None, None),
            P("section", "fsdp", None, None),
        ),
        out_specs=(
            P(("section", "fsdp"), None),
            P("section", "fsdp", None, None),
            P("section", "fsdp", None, None),
        ),
        check_vma=False,
    )
```

```python
import functools
import math

import jax
import jax.numpy as jnp
from jax import lax
from jax.experimental import pallas as pl
from jax.experimental.pallas import tpu as pltpu
from jax.sharding import PartitionSpec as P

decay_stat = 0.95
momentum_rate = 0.9
epsilon = 1e-06
lanes = 128
extra_rows = 8
ring_x = 4
ring_z = 8
pairs = ring_z // 2
roles = 4
origins = (-3, -2, -1, 0, 4, 3, 2, 1)


def shifted(block, step_x, step_z):
    route = []
    for x in range(ring_x):
        for z in range(ring_z):
            there = (x + step_x) % ring_x * ring_z + (z + step_z(z)) % ring_z
            route.append((x * ring_z + z, there))
    return lax.ppermute(block, "fsdp", route)


def outward(steps):
    return lambda z: steps if z % 2 else -steps


def scalar_sum(value):
    return jnp.sum(jnp.sum(value, axis=0, keepdims=True), axis=1, keepdims=True)


def aligned(index, multiple):
    return pl.multiple_of(index * multiple, multiple)


def in_parts(value):
    value = jnp.broadcast_to(value, (extra_rows, value.shape[1]))
    high = value.astype(jnp.bfloat16).astype(jnp.float32)
    middle = (value - high).astype(jnp.bfloat16).astype(jnp.float32)
    low = value - high - middle
    row = lax.broadcasted_iota(jnp.int32, value.shape, 0)
    parts = jnp.where(row == 0, high, jnp.where(row == 1, middle, jnp.where(row == 2, low, 0.0)))
    return parts.astype(jnp.bfloat16)


def from_parts(rows):
    wide = rows.astype(jnp.float32)
    return jnp.sum(wide, axis=0, keepdims=True)


def cut_kernel(place, grad, *rest):
    outs, sem = rest[:-1], rest[-1]
    pair, parity = place[0] % ring_z // 2, place[0] % 2
    rows_dev = grad.shape[0]
    width = outs[0].shape[1]
    body = ring_x * rows_dev
    copies = []
    for out, step in zip(outs, (2, 1 - 2 * parity, 2 * parity - 1, 0)):
        column = (pair + pairs + step) % pairs
        for x in range(ring_x):
            at = pl.ds(aligned(x * pairs + column, width), width)
            rows = pl.ds(x * rows_dev, rows_dev)
            copies.append(pltpu.make_async_copy(grad.at[:, at], out.at[rows], sem.at[len(copies)]))
            copies[-1].start()
    square = jnp.zeros((8, width), jnp.float32)
    for i, copy in enumerate(copies):
        copy.wait()
        first = i % ring_x * rows_dev
        for row in range(first, first + rows_dev, 16):
            wide = outs[i // ring_x][row : row + 16, :].astype(jnp.float32)
            square += wide[:8] * wide[:8] + wide[8:] * wide[8:]
    parts = in_parts(jnp.broadcast_to(scalar_sum(square), (1, width)))
    for out in outs:
        out[body : body + extra_rows, :] = parts


def pick_kernel(place, *refs):
    groups, outs = refs[:roles], refs[roles + 1 :]
    x = place[0] // ring_z
    body = groups[0].shape[0] - extra_rows
    rows_dev = body // ring_x
    total = sum(from_parts(group[body : body + extra_rows, :]) for group in groups)
    parts = in_parts(total)
    for d, out in enumerate(outs):
        rows = pl.ds(aligned((x + d) % ring_x, rows_dev), rows_dev)
        for i, group in enumerate(groups):
            out[i * rows_dev : (i + 1) * rows_dev, :] = group[rows, :]
        out[body : body + extra_rows, :] = parts


def root_kernel(place, own_root, partner_root, right_root, earlier, roots, right, sem):
    half = own_root.shape[1]
    parity = place[0] % 2
    own_rows, partner_rows = (pl.ds(aligned(side, half), half) for side in (parity, 1 - parity))
    bring = [
        pltpu.make_async_copy(own_root, roots.at[:, own_rows], sem.at[0]),
        pltpu.make_async_copy(partner_root, roots.at[:, partner_rows], sem.at[1]),
        pltpu.make_async_copy(right_root, right, sem.at[2]),
    ]
    for copy in bring:
        copy.start()
    for copy in bring:
        copy.wait()


def apply_kernel(clip_limit, place, *refs):
    groups = refs[: 2 * ring_x]
    root_v, right_v, blocks, payload, clip = refs[8:]
    me = place[0]
    x, z = me // ring_z, me % ring_z
    sign = 1 - 2 * (z % 2)
    row_blocks, block_size, half = right_v.shape
    owners, length, _ = payload.shape
    body = length - extra_rows
    group_body = groups[0].shape[0] - extra_rows
    rows_dev = group_body // roles

    for i, origin in enumerate(origins):
        for d in range(ring_x):
            source = (x + ring_x - d) % ring_x * ring_z + (z + ring_z + sign * origin) % ring_z
            group = groups[i // roles * ring_x + d]
            first = i % roles * rows_dev
            blocks[pl.ds(aligned(source, rows_dev), rows_dev), :] = group[first : first + rows_dev, :]
    total_sq = sum(from_parts(group[group_body : group_body + extra_rows, :]) for group in groups)
    clip_factor = jnp.minimum(1.0, clip_limit / (jnp.sqrt(total_sq) + epsilon))
    clip[...] = jnp.broadcast_to(clip_factor[:, :lanes], clip.shape)

    lane = lax.broadcasted_iota(jnp.int32, (1, lanes), 1)
    total = jnp.zeros((1, lanes), jnp.float32)
    for r in range(row_blocks):
        begin, end = r * block_size, (r + 1) * block_size
        block = blocks[begin:end, :]
        applied = jnp.dot(root_v[r], block, preferred_element_type=jnp.float32)
        precond = jnp.dot(
            applied.astype(jnp.bfloat16), right_v[r], preferred_element_type=jnp.float32
        )
        rounded = precond.astype(jnp.bfloat16)
        for f in range(begin // rows_dev, -(-end // rows_dev)):
            low, high = max(begin, f * rows_dev), min(end, (f + 1) * rows_dev)
            for c in range(half // lanes):
                at = c * rows_dev - f * rows_dev
                payload[f, at + low : at + high, :] = rounded[
                    low - begin : high - begin, c * lanes : (c + 1) * lanes
                ]
        wide = block.astype(jnp.float32)
        total += jnp.where(lane == r, scalar_sum(precond * precond), 0.0)
        total += jnp.where(lane == r + row_blocks, scalar_sum(wide * wide), 0.0)
    parts = in_parts(total)
    for f in range(owners):
        payload[f, body : body + extra_rows, :] = parts


def stat_kernel(
    place, clip, blocks, left_stat, right_stat, new_left, new_right, clip_out, stat_v, in_sem, out_sem
):
    row_blocks, half, block_size = left_stat.shape
    parity = place[0] % 2
    get, put = [], []
    for side, (stat, out) in enumerate(((left_stat, new_left), (right_stat, new_right))):
        for r in range(row_blocks):
            i = side * row_blocks + r
            get.append(pltpu.make_async_copy(stat.at[r], stat_v.at[i], in_sem.at[i]))
            put.append(pltpu.make_async_copy(stat_v.at[i], out.at[r], out_sem.at[i]))
            get[-1].start()
    clip_out[...] = clip[...]
    factor = clip[0:1, 0:1]
    coeff = (1.0 - decay_stat) * factor * factor
    for r in range(row_blocks):
        begin = r * block_size
        block = blocks[begin : begin + block_size, :]
        rows = blocks[pl.ds(pl.multiple_of(begin + parity * half, half), half), :]
        gram = lax.dot_general(
            rows, block, (((1,), (1,)), ((), ())), preferred_element_type=jnp.float32
        )
        get[r].wait()
        stat_v[r] = decay_stat * stat_v[r] + coeff * gram
        put[r].start()
    for r in range(row_blocks):
        i = row_blocks + r
        get[i].wait()
        for side in range(2):

            @pl.when(parity == side)
            def _():
                block = blocks[r * block_size : (r + 1) * block_size, :]
                gram = lax.dot_general(
                    block[:, side * half : (side + 1) * half], block,
                    (((0,), (0,)), ((), ())), preferred_element_type=jnp.float32,
                )
                stat_v[i] = decay_stat * stat_v[i] + coeff * gram

        put[i].start()
    for copy in put:
        copy.wait()


def finish_kernel(
    row_blocks, block_size, place, back, clip, momentum, new_momentum,
    back_v, norm_v, clip_v, momentum_v, back_sem, norm_sem, clip_sem, in_sem, out_sem,
):
    me = place[0]
    rows_dev, all_cols = momentum.shape
    owners, length, _ = back.shape
    pieces = out_sem.shape[0]
    width = all_cols // pieces
    share = owners // pieces
    columns = all_cols // owners
    body = length - extra_rows

    first_here = [
        pltpu.make_async_copy(back.at[:, pl.ds(body, extra_rows)], norm_v, norm_sem),
        pltpu.make_async_copy(clip, clip_v, clip_sem),
    ]
    for copy in first_here:
        copy.start()
    get_back, get_momentum, put_momentum = [], [], []
    for q in range(pieces):
        some, part = pl.ds(q * share, share), pl.ds(q * width, width)
        rows = pl.ds(0, body)
        get_back.append(
            pltpu.make_async_copy(back.at[some, rows], back_v.at[some], back_sem.at[q])
        )
        get_momentum.append(
            pltpu.make_async_copy(momentum.at[:, part], momentum_v.at[:, part], in_sem.at[q])
        )
        put_momentum.append(
            pltpu.make_async_copy(momentum_v.at[:, part], new_momentum.at[:, part], out_sem.at[q])
        )
        get_back[-1].start()
        get_momentum[-1].start()
    for copy in first_here:
        copy.wait()

    parts = norm_v[...].astype(jnp.float32)
    values = parts[:, 0, :] + parts[:, 1, :] + parts[:, 2, :]
    lane = lax.broadcasted_iota(jnp.int32, values.shape, 1)
    source = lax.broadcasted_iota(jnp.int32, values.shape, 0)
    paired = jnp.where(
        source % 2 == 0, pltpu.roll(values, owners - 1, 0), pltpu.roll(values, 1, 0)
    )
    pnorm = values + paired
    gnorm = pltpu.roll(values, lanes - row_blocks, 1)
    scale = clip_v[0:1, :] * jnp.sqrt(gnorm) / (jnp.sqrt(pnorm) + epsilon)
    first = me * rows_dev // block_size
    until = (first + 1) * block_size - me * rows_dev
    upper = jnp.sum(jnp.where(lane == first, scale, 0.0), axis=1, keepdims=True)
    lower = jnp.sum(
        jnp.where((lane == first + 1) & (lane < row_blocks), scale, 0.0), axis=1, keepdims=True
    )
    in_upper = lax.broadcasted_iota(jnp.int32, (rows_dev, lanes), 0) < until
    for q in range(pieces):
        get_back[q].wait()
        get_momentum[q].wait()
        for s in range(q * share, (q + 1) * share):
            row_scale = jnp.where(in_upper, upper[s : s + 1], lower[s : s + 1])
            for c in range(columns // lanes):
                at = pl.ds(s * columns + c * lanes, lanes)
                moved = back_v[s, c * rows_dev : (c + 1) * rows_dev, :].astype(jnp.float32)
                momentum_v[:, at] = momentum_rate * momentum_v[:, at] + row_scale * moved
        put_momentum[q].start()
    for copy in put_momentum:
        copy.wait()


def keep_in_hbm(array):
    return pltpu.with_memory_space_constraint(array, pltpu.HBM)


def local(grad, momentum, left_stat, right_stat, left_root, right_root):
    owners = ring_x * ring_z
    place = lax.axis_index("fsdp").astype(jnp.int32).reshape(1)
    rows_dev, all_cols = grad.shape
    row_blocks, _, half, block_size = left_stat.shape
    all_rows = rows_dev * owners
    clip_limit = 0.5 * math.sqrt(all_rows * all_cols)
    length = rows_dev * half // lanes + extra_rows
    smem = pl.BlockSpec(memory_space=pltpu.SMEM)
    in_hbm = pl.BlockSpec(memory_space=pltpu.HBM)
    in_vmem = pl.BlockSpec(memory_space=pltpu.VMEM)
    some_vmem = pltpu.CompilerParams(vmem_limit_bytes=16 << 20)
    flops = row_blocks * 2 * half * block_size * block_size
    dma = pltpu.SemaphoreType.DMA

    def cost(flops, megabytes):
        return pl.CostEstimate(flops=flops, bytes_accessed=megabytes << 20, transcendentals=0)

    def array(*shape, dtype=jnp.bfloat16):
        return jax.ShapeDtypeStruct(shape, dtype)

    left_root = left_root.reshape(row_blocks, half, block_size)
    right_root = right_root.reshape(row_blocks, block_size, half)
    left_stat = left_stat.reshape(row_blocks, half, block_size)
    right_stat = right_stat.reshape(row_blocks, half, block_size)
    group = array(ring_x * rows_dev + extra_rows, block_size)
    stat = array(row_blocks, half, block_size, dtype=jnp.float32)
    wide = array(rows_dev, all_cols, dtype=jnp.float32)
    still = lambda z: 0
    to_partner = outward(-1)

    partner_root = shifted(left_root, 0, to_partner)
    *sent, own = pl.pallas_call(
        cut_kernel,
        out_shape=[group] * roles,
        in_specs=[smem, in_hbm],
        out_specs=[in_vmem] * roles,
        scratch_shapes=[dma((roles * ring_x,))],
        compiler_params=some_vmem,
        cost_estimate=cost(0, 1),
        name="cut",
    )(place, keep_in_hbm(grad))
    far, same, cross = (shifted(block, 0, outward(n)) for block, n in zip(sent, (3, -2, 1)))
    parts = pl.pallas_call(
        pick_kernel,
        out_shape=[group] * ring_x,
        in_specs=[smem] + [in_vmem] * roles + [in_hbm],
        out_specs=[in_vmem] * ring_x,
        compiler_params=some_vmem,
        cost_estimate=cost(0, 2),
        name="pick",
    )(place, far, same, cross, own, partner_root)
    near = [parts[0]] + [shifted(parts[d], d, still) for d in range(1, ring_x)]
    swapped = [shifted(parts[d], d, to_partner) for d in range(ring_x) if d != 2]
    swapped.insert(2, shifted(near[2], 0, to_partner))

    roots, right = pl.pallas_call(
        root_kernel,
        out_shape=[
            array(row_blocks, block_size, block_size),
            array(row_blocks, block_size, half),
        ],
        in_specs=[smem] + [in_hbm] * 4,
        out_specs=[in_vmem] * 2,
        scratch_shapes=[dma((3,))],
        compiler_params=some_vmem,
        cost_estimate=cost(0, 4),
        name="roots",
    )(place, keep_in_hbm(left_root), partner_root, keep_in_hbm(right_root), near[2])

    blocks, payload, clip = pl.pallas_call(
        functools.partial(apply_kernel, clip_limit),
        out_shape=[
            array(all_rows, block_size),
            array(owners, length, lanes),
            array(8, lanes, dtype=jnp.float32),
        ],
        in_specs=[smem] + [in_vmem] * (2 * ring_x + 2),
        out_specs=[in_vmem] * 3,
        compiler_params=some_vmem,
        cost_estimate=cost(3 * flops, 6),
        name="apply",
    )(place, *near, *swapped, roots, right)
    back = lax.all_to_all(payload, "fsdp", split_axis=0, concat_axis=0, tiled=True)
    new_left, new_right, clip = pl.pallas_call(
        stat_kernel,
        out_shape=[stat] * 2 + [array(8, lanes, dtype=jnp.float32)],
        in_specs=[smem, in_vmem, in_vmem, in_hbm, in_hbm],
        out_specs=[in_hbm, in_hbm, in_vmem],
        scratch_shapes=[
            pltpu.VMEM((2 * row_blocks, half, block_size), jnp.float32),
            dma((2 * row_blocks,)),
            dma((2 * row_blocks,)),
        ],
        compiler_params=some_vmem,
        cost_estimate=cost(2 * flops, 8),
        name="statistics",
    )(place, clip, blocks, keep_in_hbm(left_stat), keep_in_hbm(right_stat))

    pieces = 8
    new_momentum = pl.pallas_call(
        functools.partial(finish_kernel, row_blocks, block_size),
        out_shape=wide,
        in_specs=[smem] + [in_hbm] * 3,
        out_specs=in_hbm,
        scratch_shapes=[
            pltpu.VMEM((owners, length - extra_rows, lanes), jnp.bfloat16),
            pltpu.VMEM((owners, extra_rows, lanes), jnp.bfloat16),
            pltpu.VMEM((8, lanes), jnp.float32),
            pltpu.VMEM((rows_dev, all_cols), jnp.float32),
            dma((pieces,)),
            dma,
            dma,
            dma((pieces,)),
            dma((pieces,)),
        ],
        compiler_params=some_vmem,
        cost_estimate=cost(1 << 22, 4),
        name="finish",
    )(place, back, clip, keep_in_hbm(momentum))
    shape = (row_blocks, 1, half, block_size)
    return (new_momentum, new_left.reshape(shape), new_right.reshape(shape))


def solution(mesh):
    return jax.shard_map(
        local,
        mesh=mesh,
        in_specs=(
            P(("section", "fsdp"), None),
            P(("section", "fsdp"), None),
            P("section", "fsdp", None, None),
            P("section", "fsdp", None, None),
            P("section", "fsdp", None, None),
            P("section", "fsdp", None, None),
        ),
        out_specs=(
            P(("section", "fsdp"), None),
            P("section", "fsdp", None, None),
            P("section", "fsdp", None, None),
        ),
        check_vma=False,
    )
```

```python
import functools
import math

import jax
import jax.numpy as jnp
from jax import lax
from jax.experimental import pallas as pl
from jax.experimental.pallas import tpu as pltpu
from jax.sharding import PartitionSpec as P

decay_stat = 0.95
momentum_rate = 0.9
epsilon = 1e-06
lanes = 128
extra_rows = 8
ring_x = 4
ring_z = 8
pairs = ring_z // 2
roles = 4
origins = (-3, -2, -1, 0, 4, 3, 2, 1)


def shifted(block, step_x, step_z):
    route = []
    for x in range(ring_x):
        for z in range(ring_z):
            there = (x + step_x) % ring_x * ring_z + (z + step_z(z)) % ring_z
            route.append((x * ring_z + z, there))
    return lax.ppermute(block, "fsdp", route)


def outward(steps):
    return lambda z: steps if z % 2 else -steps


def scalar_sum(value):
    return jnp.sum(jnp.sum(value, axis=0, keepdims=True), axis=1, keepdims=True)


def aligned(index, multiple):
    return pl.multiple_of(index * multiple, multiple)


def in_parts(value):
    value = jnp.broadcast_to(value, (extra_rows, value.shape[1]))
    high = value.astype(jnp.bfloat16).astype(jnp.float32)
    middle = (value - high).astype(jnp.bfloat16).astype(jnp.float32)
    low = value - high - middle
    row = lax.broadcasted_iota(jnp.int32, value.shape, 0)
    parts = jnp.where(row == 0, high, jnp.where(row == 1, middle, jnp.where(row == 2, low, 0.0)))
    return parts.astype(jnp.bfloat16)


def from_parts(rows):
    wide = rows.astype(jnp.float32)
    return jnp.sum(wide, axis=0, keepdims=True)


def cut_kernel(place, grad, left_root, *rest):
    outs, early_root, sem, root_sem = rest[:-3], rest[-3], rest[-2], rest[-1]
    early = pl.ds(0, early_root.shape[0])
    get_root = pltpu.make_async_copy(left_root.at[early], early_root, root_sem)
    pair, parity = place[0] % ring_z // 2, place[0] % 2
    rows_dev = grad.shape[0]
    width = outs[0].shape[1]
    body = ring_x * rows_dev
    copies = []
    for out, step in zip(outs, (2, 1 - 2 * parity, 2 * parity - 1, 0)):
        column = (pair + pairs + step) % pairs
        for x in range(ring_x):
            at = pl.ds(aligned(x * pairs + column, width), width)
            rows = pl.ds(x * rows_dev, rows_dev)
            copies.append(pltpu.make_async_copy(grad.at[:, at], out.at[rows], sem.at[len(copies)]))
            copies[-1].start()
    get_root.start()
    square = jnp.zeros((8, width), jnp.float32)
    for i, copy in enumerate(copies):
        copy.wait()
        first = i % ring_x * rows_dev
        for row in range(first, first + rows_dev, 16):
            wide = outs[i // ring_x][row : row + 16, :].astype(jnp.float32)
            square += wide[:8] * wide[:8] + wide[8:] * wide[8:]
    parts = in_parts(jnp.broadcast_to(scalar_sum(square), (1, width)))
    for out in outs:
        out[body : body + extra_rows, :] = parts
    get_root.wait()


def pick_kernel(place, *refs):
    groups, last_root, outs = refs[:roles], refs[roles], refs[roles + 2 :]
    half = last_root.shape[0]
    outs[0][outs[0].shape[0] - half :, :] = last_root[...]
    x = place[0] // ring_z
    body = groups[0].shape[0] - extra_rows
    rows_dev = body // ring_x
    total = sum(from_parts(group[body : body + extra_rows, :]) for group in groups)
    parts = in_parts(total)
    for d, out in enumerate(outs):
        rows = pl.ds(aligned((x + d) % ring_x, rows_dev), rows_dev)
        for i, group in enumerate(groups):
            out[i * rows_dev : (i + 1) * rows_dev, :] = group[rows, :]
        out[body : body + extra_rows, :] = parts


def root_kernel(
    place, own_root, partner_early, message, right_root, earlier, roots, right, sem
):
    row_blocks, half, _ = own_root.shape
    early = row_blocks - 1
    partner_last = message.at[pl.ds(message.shape[0] - half, half)]
    parity = place[0] % 2
    own_rows, partner_rows = (pl.ds(aligned(side, half), half) for side in (parity, 1 - parity))
    bring = [
        pltpu.make_async_copy(own_root, roots.at[:, own_rows], sem.at[0]),
        pltpu.make_async_copy(partner_early, roots.at[pl.ds(0, early), partner_rows], sem.at[1]),
        pltpu.make_async_copy(partner_last, roots.at[early, partner_rows], sem.at[2]),
        pltpu.make_async_copy(right_root, right, sem.at[3]),
    ]
    for copy in bring:
        copy.start()
    for copy in bring:
        copy.wait()


def apply_kernel(clip_limit, place, *refs):
    groups = refs[: 2 * ring_x]
    root_v, right_v, blocks, payload, clip = refs[8:]
    me = place[0]
    x, z = me // ring_z, me % ring_z
    sign = 1 - 2 * (z % 2)
    row_blocks, block_size, half = right_v.shape
    owners, length, _ = payload.shape
    body = length - extra_rows
    group_body = groups[1].shape[0] - extra_rows
    rows_dev = group_body // roles

    for i, origin in enumerate(origins):
        for d in range(ring_x):
            source = (x + ring_x - d) % ring_x * ring_z + (z + ring_z + sign * origin) % ring_z
            group = groups[i // roles * ring_x + d]
            first = i % roles * rows_dev
            blocks[pl.ds(aligned(source, rows_dev), rows_dev), :] = group[first : first + rows_dev, :]
    total_sq = sum(from_parts(group[group_body : group_body + extra_rows, :]) for group in groups)
    clip_factor = jnp.minimum(1.0, clip_limit / (jnp.sqrt(total_sq) + epsilon))
    clip[...] = jnp.broadcast_to(clip_factor[:, :lanes], clip.shape)

    lane = lax.broadcasted_iota(jnp.int32, (1, lanes), 1)
    total = jnp.zeros((1, lanes), jnp.float32)
    for r in range(row_blocks):
        begin, end = r * block_size, (r + 1) * block_size
        block = blocks[begin:end, :]
        applied = jnp.dot(root_v[r], block, preferred_element_type=jnp.float32)
        precond = jnp.dot(
            applied.astype(jnp.bfloat16), right_v[r], preferred_element_type=jnp.float32
        )
        rounded = precond.astype(jnp.bfloat16)
        for f in range(begin // rows_dev, -(-end // rows_dev)):
            low, high = max(begin, f * rows_dev), min(end, (f + 1) * rows_dev)
            for c in range(half // lanes):
                at = c * rows_dev - f * rows_dev
                payload[f, at + low : at + high, :] = rounded[
                    low - begin : high - begin, c * lanes : (c + 1) * lanes
                ]
        wide = block.astype(jnp.float32)
        total += jnp.where(lane == r, scalar_sum(precond * precond), 0.0)
        total += jnp.where(lane == r + row_blocks, scalar_sum(wide * wide), 0.0)
    parts = in_parts(total)
    for f in range(owners):
        payload[f, body : body + extra_rows, :] = parts


def stat_kernel(
    place, clip, blocks, left_stat, right_stat, new_left, new_right, clip_out, stat_v, in_sem, out_sem
):
    row_blocks, half, block_size = left_stat.shape
    parity = place[0] % 2
    get, put = [], []
    for side, (stat, out) in enumerate(((left_stat, new_left), (right_stat, new_right))):
        for r in range(row_blocks):
            i = side * row_blocks + r
            get.append(pltpu.make_async_copy(stat.at[r], stat_v.at[i], in_sem.at[i]))
            put.append(pltpu.make_async_copy(stat_v.at[i], out.at[r], out_sem.at[i]))
            get[-1].start()
    clip_out[...] = clip[...]
    factor = clip[0:1, 0:1]
    coeff = (1.0 - decay_stat) * factor * factor
    for r in range(row_blocks):
        begin = r * block_size
        block = blocks[begin : begin + block_size, :]
        rows = blocks[pl.ds(pl.multiple_of(begin + parity * half, half), half), :]
        gram = lax.dot_general(
            rows, block, (((1,), (1,)), ((), ())), preferred_element_type=jnp.float32
        )
        get[r].wait()
        stat_v[r] = decay_stat * stat_v[r] + coeff * gram
        put[r].start()
    for r in range(row_blocks):
        i = row_blocks + r
        get[i].wait()
        for side in range(2):

            @pl.when(parity == side)
            def _():
                block = blocks[r * block_size : (r + 1) * block_size, :]
                gram = lax.dot_general(
                    block[:, side * half : (side + 1) * half], block,
                    (((0,), (0,)), ((), ())), preferred_element_type=jnp.float32,
                )
                stat_v[i] = decay_stat * stat_v[i] + coeff * gram

        put[i].start()
    for copy in put:
        copy.wait()


def finish_kernel(
    row_blocks, block_size, place, back, clip, momentum, new_momentum,
    back_v, norm_v, clip_v, momentum_v, back_sem, norm_sem, clip_sem, in_sem, out_sem,
):
    me = place[0]
    rows_dev, all_cols = momentum.shape
    owners, length, _ = back.shape
    pieces = out_sem.shape[0]
    width = all_cols // pieces
    share = owners // pieces
    columns = all_cols // owners
    body = length - extra_rows

    first_here = [
        pltpu.make_async_copy(back.at[:, pl.ds(body, extra_rows)], norm_v, norm_sem),
        pltpu.make_async_copy(clip, clip_v, clip_sem),
    ]
    for copy in first_here:
        copy.start()
    get_back, get_momentum, put_momentum = [], [], []
    for q in range(pieces):
        some, part = pl.ds(q * share, share), pl.ds(q * width, width)
        rows = pl.ds(0, body)
        get_back.append(
            pltpu.make_async_copy(back.at[some, rows], back_v.at[some], back_sem.at[q])
        )
        get_momentum.append(
            pltpu.make_async_copy(momentum.at[:, part], momentum_v.at[:, part], in_sem.at[q])
        )
        put_momentum.append(
            pltpu.make_async_copy(momentum_v.at[:, part], new_momentum.at[:, part], out_sem.at[q])
        )
        get_back[-1].start()
        get_momentum[-1].start()
    for copy in first_here:
        copy.wait()

    parts = norm_v[...].astype(jnp.float32)
    values = parts[:, 0, :] + parts[:, 1, :] + parts[:, 2, :]
    lane = lax.broadcasted_iota(jnp.int32, values.shape, 1)
    source = lax.broadcasted_iota(jnp.int32, values.shape, 0)
    paired = jnp.where(
        source % 2 == 0, pltpu.roll(values, owners - 1, 0), pltpu.roll(values, 1, 0)
    )
    pnorm = values + paired
    gnorm = pltpu.roll(values, lanes - row_blocks, 1)
    scale = clip_v[0:1, :] * jnp.sqrt(gnorm) / (jnp.sqrt(pnorm) + epsilon)
    first = me * rows_dev // block_size
    until = (first + 1) * block_size - me * rows_dev
    upper = jnp.sum(jnp.where(lane == first, scale, 0.0), axis=1, keepdims=True)
    lower = jnp.sum(
        jnp.where((lane == first + 1) & (lane < row_blocks), scale, 0.0), axis=1, keepdims=True
    )
    in_upper = lax.broadcasted_iota(jnp.int32, (rows_dev, lanes), 0) < until
    for q in range(pieces):
        get_back[q].wait()
        get_momentum[q].wait()
        for s in range(q * share, (q + 1) * share):
            row_scale = jnp.where(in_upper, upper[s : s + 1], lower[s : s + 1])
            for c in range(columns // lanes):
                at = pl.ds(s * columns + c * lanes, lanes)
                moved = back_v[s, c * rows_dev : (c + 1) * rows_dev, :].astype(jnp.float32)
                momentum_v[:, at] = momentum_rate * momentum_v[:, at] + row_scale * moved
        put_momentum[q].start()
    for copy in put_momentum:
        copy.wait()


def keep_in_hbm(array):
    return pltpu.with_memory_space_constraint(array, pltpu.HBM)


def local(grad, momentum, left_stat, right_stat, left_root, right_root):
    owners = ring_x * ring_z
    place = lax.axis_index("fsdp").astype(jnp.int32).reshape(1)
    rows_dev, all_cols = grad.shape
    row_blocks, _, half, block_size = left_stat.shape
    all_rows = rows_dev * owners
    clip_limit = 0.5 * math.sqrt(all_rows * all_cols)
    length = rows_dev * half // lanes + extra_rows
    smem = pl.BlockSpec(memory_space=pltpu.SMEM)
    in_hbm = pl.BlockSpec(memory_space=pltpu.HBM)
    in_vmem = pl.BlockSpec(memory_space=pltpu.VMEM)
    some_vmem = pltpu.CompilerParams(vmem_limit_bytes=16 << 20)
    flops = row_blocks * 2 * half * block_size * block_size
    dma = pltpu.SemaphoreType.DMA

    def cost(flops, megabytes):
        return pl.CostEstimate(flops=flops, bytes_accessed=megabytes << 20, transcendentals=0)

    def array(*shape, dtype=jnp.bfloat16):
        return jax.ShapeDtypeStruct(shape, dtype)

    left_root = left_root.reshape(row_blocks, half, block_size)
    right_root = right_root.reshape(row_blocks, block_size, half)
    left_stat = left_stat.reshape(row_blocks, half, block_size)
    right_stat = right_stat.reshape(row_blocks, half, block_size)
    group = array(ring_x * rows_dev + extra_rows, block_size)
    stat = array(row_blocks, half, block_size, dtype=jnp.float32)
    wide = array(rows_dev, all_cols, dtype=jnp.float32)
    message_rows = -(-group.shape[0] // 16) * 16 + half
    still = lambda z: 0
    to_partner = outward(-1)

    *sent, own, early_root = pl.pallas_call(
        cut_kernel,
        out_shape=[group] * roles + [array(row_blocks - 1, half, block_size)],
        in_specs=[smem, in_hbm, in_hbm],
        out_specs=[in_vmem] * (roles + 1),
        scratch_shapes=[dma((roles * ring_x,)), dma],
        compiler_params=some_vmem,
        cost_estimate=cost(0, 1),
        name="cut",
    )(place, keep_in_hbm(grad), keep_in_hbm(left_root))
    partner_early = shifted(early_root, 0, to_partner)
    far, same, cross = (shifted(block, 0, outward(n)) for block, n in zip(sent, (3, -2, 1)))
    parts = pl.pallas_call(
        pick_kernel,
        out_shape=[array(message_rows, block_size)] + [group] * (ring_x - 1),
        in_specs=[smem] + [in_vmem] * (roles + 1) + [in_hbm],
        out_specs=[in_vmem] * ring_x,
        compiler_params=some_vmem,
        cost_estimate=cost(0, 2),
        name="pick",
    )(place, far, same, cross, own, left_root[row_blocks - 1], partner_early)
    near = [parts[0]] + [shifted(parts[d], d, still) for d in range(1, ring_x)]
    swapped = [shifted(parts[d], d, to_partner) for d in range(ring_x) if d != 2]
    swapped.insert(2, shifted(near[2], 0, to_partner))

    roots, right = pl.pallas_call(
        root_kernel,
        out_shape=[
            array(row_blocks, block_size, block_size),
            array(row_blocks, block_size, half),
        ],
        in_specs=[smem] + [in_hbm] * 5,
        out_specs=[in_vmem] * 2,
        scratch_shapes=[dma((4,))],
        compiler_params=some_vmem,
        cost_estimate=cost(0, 4),
        name="roots",
    )(
        place, keep_in_hbm(left_root), partner_early, swapped[0], keep_in_hbm(right_root), near[2]
    )

    blocks, payload, clip = pl.pallas_call(
        functools.partial(apply_kernel, clip_limit),
        out_shape=[
            array(all_rows, block_size),
            array(owners, length, lanes),
            array(8, lanes, dtype=jnp.float32),
        ],
        in_specs=[smem] + [in_vmem] * (2 * ring_x + 2),
        out_specs=[in_vmem] * 3,
        compiler_params=some_vmem,
        cost_estimate=cost(3 * flops, 6),
        name="apply",
    )(place, *near, *swapped, roots, right)
    back = lax.all_to_all(payload, "fsdp", split_axis=0, concat_axis=0, tiled=True)
    new_left, new_right, clip = pl.pallas_call(
        stat_kernel,
        out_shape=[stat] * 2 + [array(8, lanes, dtype=jnp.float32)],
        in_specs=[smem, in_vmem, in_vmem, in_hbm, in_hbm],
        out_specs=[in_hbm, in_hbm, in_vmem],
        scratch_shapes=[
            pltpu.VMEM((2 * row_blocks, half, block_size), jnp.float32),
            dma((2 * row_blocks,)),
            dma((2 * row_blocks,)),
        ],
        compiler_params=some_vmem,
        cost_estimate=cost(2 * flops, 8),
        name="statistics",
    )(place, clip, blocks, keep_in_hbm(left_stat), keep_in_hbm(right_stat))

    pieces = 8
    new_momentum = pl.pallas_call(
        functools.partial(finish_kernel, row_blocks, block_size),
        out_shape=wide,
        in_specs=[smem] + [in_hbm] * 3,
        out_specs=in_hbm,
        scratch_shapes=[
            pltpu.VMEM((owners, length - extra_rows, lanes), jnp.bfloat16),
            pltpu.VMEM((owners, extra_rows, lanes), jnp.bfloat16),
            pltpu.VMEM((8, lanes), jnp.float32),
            pltpu.VMEM((rows_dev, all_cols), jnp.float32),
            dma((pieces,)),
            dma,
            dma,
            dma((pieces,)),
            dma((pieces,)),
        ],
        compiler_params=some_vmem,
        cost_estimate=cost(1 << 22, 4),
        name="finish",
    )(place, back, clip, keep_in_hbm(momentum))
    shape = (row_blocks, 1, half, block_size)
    return (new_momentum, new_left.reshape(shape), new_right.reshape(shape))


def solution(mesh):
    return jax.shard_map(
        local,
        mesh=mesh,
        in_specs=(
            P(("section", "fsdp"), None),
            P(("section", "fsdp"), None),
            P("section", "fsdp", None, None),
            P("section", "fsdp", None, None),
            P("section", "fsdp", None, None),
            P("section", "fsdp", None, None),
        ),
        out_specs=(
            P(("section", "fsdp"), None),
            P("section", "fsdp", None, None),
            P("section", "fsdp", None, None),
        ),
        check_vma=False,
    )
```

```python
import functools
import math

import jax
import jax.numpy as jnp
from jax import lax
from jax.experimental import pallas as pl
from jax.experimental.pallas import tpu as pltpu
from jax.sharding import PartitionSpec as P

decay_stat = 0.95
momentum_rate = 0.9
epsilon = 1e-06
lanes = 128
extra_rows = 8
ring_x = 4
ring_z = 8
pairs = ring_z // 2
roles = 4
origins = (-3, -2, -1, 0, 4, 3, 2, 1)


def shifted(block, step_x, step_z):
    route = []
    for x in range(ring_x):
        for z in range(ring_z):
            there = (x + step_x) % ring_x * ring_z + (z + step_z(z)) % ring_z
            route.append((x * ring_z + z, there))
    return lax.ppermute(block, "fsdp", route)


def outward(steps):
    return lambda z: steps if z % 2 else -steps


def scalar_sum(value):
    return jnp.sum(jnp.sum(value, axis=0, keepdims=True), axis=1, keepdims=True)


def aligned(index, multiple):
    return pl.multiple_of(index * multiple, multiple)


def in_parts(value):
    value = jnp.broadcast_to(value, (extra_rows, value.shape[1]))
    high = value.astype(jnp.bfloat16).astype(jnp.float32)
    middle = (value - high).astype(jnp.bfloat16).astype(jnp.float32)
    low = value - high - middle
    row = lax.broadcasted_iota(jnp.int32, value.shape, 0)
    parts = jnp.where(row == 0, high, jnp.where(row == 1, middle, jnp.where(row == 2, low, 0.0)))
    return parts.astype(jnp.bfloat16)


def from_parts(rows):
    wide = rows.astype(jnp.float32)
    return jnp.sum(wide, axis=0, keepdims=True)


def cut_kernel(place, grad, *rest):
    outs, sem = rest[:-1], rest[-1]
    pair, parity = place[0] % ring_z // 2, place[0] % 2
    rows_dev = grad.shape[0]
    width = outs[0].shape[1]
    body = ring_x * rows_dev
    copies = []
    for out, step in zip(outs, (2, 1 - 2 * parity, 2 * parity - 1, 0)):
        column = (pair + pairs + step) % pairs
        for x in range(ring_x):
            at = pl.ds(aligned(x * pairs + column, width), width)
            rows = pl.ds(x * rows_dev, rows_dev)
            copies.append(pltpu.make_async_copy(grad.at[:, at], out.at[rows], sem.at[len(copies)]))
            copies[-1].start()
    square = jnp.zeros((8, width), jnp.float32)
    for i, copy in enumerate(copies):
        copy.wait()
        first = i % ring_x * rows_dev
        for row in range(first, first + rows_dev, 16):
            wide = outs[i // ring_x][row : row + 16, :].astype(jnp.float32)
            square += wide[:8] * wide[:8] + wide[8:] * wide[8:]
    parts = in_parts(jnp.broadcast_to(scalar_sum(square), (1, width)))
    for out in outs:
        out[body : body + extra_rows, :] = parts


def pick_kernel(place, *refs):
    groups, outs = refs[:roles], refs[roles + 1 :]
    x = place[0] // ring_z
    body = groups[0].shape[0] - extra_rows
    rows_dev = body // ring_x
    total = sum(from_parts(group[body : body + extra_rows, :]) for group in groups)
    parts = in_parts(total)
    for d, out in enumerate(outs):
        rows = pl.ds(aligned((x + d) % ring_x, rows_dev), rows_dev)
        for i, group in enumerate(groups):
            out[i * rows_dev : (i + 1) * rows_dev, :] = group[rows, :]
        out[body : body + extra_rows, :] = parts


def root_kernel(place, own_root, partner_root, right_root, earlier, roots, right, sem):
    half = own_root.shape[1]
    parity = place[0] % 2
    own_rows, partner_rows = (pl.ds(aligned(side, half), half) for side in (parity, 1 - parity))
    bring = [
        pltpu.make_async_copy(own_root, roots.at[:, own_rows], sem.at[0]),
        pltpu.make_async_copy(partner_root, roots.at[:, partner_rows], sem.at[1]),
        pltpu.make_async_copy(right_root, right, sem.at[2]),
    ]
    for copy in bring:
        copy.start()
    for copy in bring:
        copy.wait()


def apply_kernel(clip_limit, place, *refs):
    groups = refs[: 2 * ring_x]
    root_v, right_v, blocks, payload, clip = refs[8:]
    me = place[0]
    x, z = me // ring_z, me % ring_z
    sign = 1 - 2 * (z % 2)
    row_blocks, block_size, half = right_v.shape
    owners, length, _ = payload.shape
    body = length - extra_rows
    group_body = groups[0].shape[0] - extra_rows
    rows_dev = group_body // roles

    for i, origin in enumerate(origins):
        for d in range(ring_x):
            source = (x + ring_x - d) % ring_x * ring_z + (z + ring_z + sign * origin) % ring_z
            group = groups[i // roles * ring_x + d]
            first = i % roles * rows_dev
            blocks[pl.ds(aligned(source, rows_dev), rows_dev), :] = group[first : first + rows_dev, :]
    total_sq = sum(from_parts(group[group_body : group_body + extra_rows, :]) for group in groups)
    clip_factor = jnp.minimum(1.0, clip_limit / (jnp.sqrt(total_sq) + epsilon))
    clip[...] = jnp.broadcast_to(clip_factor[:, :lanes], clip.shape)

    lane = lax.broadcasted_iota(jnp.int32, (1, lanes), 1)
    total = jnp.zeros((1, lanes), jnp.float32)
    for r in range(row_blocks):
        begin, end = r * block_size, (r + 1) * block_size
        block = blocks[begin:end, :]
        applied = jnp.dot(root_v[r], block, preferred_element_type=jnp.float32)
        precond = jnp.dot(
            applied.astype(jnp.bfloat16), right_v[r], preferred_element_type=jnp.float32
        )
        rounded = precond.astype(jnp.bfloat16)
        for f in range(begin // rows_dev, -(-end // rows_dev)):
            low, high = max(begin, f * rows_dev), min(end, (f + 1) * rows_dev)
            for c in range(half // lanes):
                at = c * rows_dev - f * rows_dev
                payload[f, at + low : at + high, :] = rounded[
                    low - begin : high - begin, c * lanes : (c + 1) * lanes
                ]
        wide = block.astype(jnp.float32)
        total += jnp.where(lane == r, scalar_sum(precond * precond), 0.0)
        total += jnp.where(lane == r + row_blocks, scalar_sum(wide * wide), 0.0)
    parts = in_parts(total)
    for f in range(owners):
        payload[f, body : body + extra_rows, :] = parts


def stat_kernel(
    place, clip, blocks, left_stat, right_stat, new_left, new_right, clip_out, stat_v, in_sem, out_sem
):
    row_blocks, half, block_size = left_stat.shape
    parity = place[0] % 2
    get, put = [], []
    for side, (stat, out) in enumerate(((left_stat, new_left), (right_stat, new_right))):
        for r in range(row_blocks):
            i = side * row_blocks + r
            get.append(pltpu.make_async_copy(stat.at[r], stat_v.at[i], in_sem.at[i]))
            put.append(pltpu.make_async_copy(stat_v.at[i], out.at[r], out_sem.at[i]))
            get[-1].start()
    clip_out[...] = clip[...]
    factor = clip[0:1, 0:1]
    coeff = (1.0 - decay_stat) * factor * factor
    for r in range(row_blocks):
        begin = r * block_size
        block = blocks[begin : begin + block_size, :]
        rows = blocks[pl.ds(pl.multiple_of(begin + parity * half, half), half), :]
        gram = lax.dot_general(
            rows, block, (((1,), (1,)), ((), ())), preferred_element_type=jnp.float32
        )
        get[r].wait()
        stat_v[r] = decay_stat * stat_v[r] + coeff * gram
        put[r].start()
    for r in range(row_blocks):
        i = row_blocks + r
        get[i].wait()
        for side in range(2):

            @pl.when(parity == side)
            def _():
                block = blocks[r * block_size : (r + 1) * block_size, :]
                gram = lax.dot_general(
                    block[:, side * half : (side + 1) * half], block,
                    (((0,), (0,)), ((), ())), preferred_element_type=jnp.float32,
                )
                stat_v[i] = decay_stat * stat_v[i] + coeff * gram

        put[i].start()
    for copy in put:
        copy.wait()


def finish_kernel(
    row_blocks, block_size, place, back, clip, momentum, new_momentum,
    back_v, norm_v, clip_v, momentum_v, back_sem, norm_sem, clip_sem, in_sem, out_sem,
):
    me = place[0]
    rows_dev, all_cols = momentum.shape
    owners, length, _ = back.shape
    pieces = out_sem.shape[0]
    width = all_cols // pieces
    share = owners // pieces
    columns = all_cols // owners
    body = length - extra_rows

    first_here = [
        pltpu.make_async_copy(back.at[:, pl.ds(body, extra_rows)], norm_v, norm_sem),
        pltpu.make_async_copy(clip, clip_v, clip_sem),
    ]
    for copy in first_here:
        copy.start()
    get_back, get_momentum, put_momentum = [], [], []
    for q in range(pieces):
        some, part = pl.ds(q * share, share), pl.ds(q * width, width)
        rows = pl.ds(0, body)
        get_back.append(
            pltpu.make_async_copy(back.at[some, rows], back_v.at[some], back_sem.at[q])
        )
        get_momentum.append(
            pltpu.make_async_copy(momentum.at[:, part], momentum_v.at[:, part], in_sem.at[q])
        )
        put_momentum.append(
            pltpu.make_async_copy(momentum_v.at[:, part], new_momentum.at[:, part], out_sem.at[q])
        )
        get_back[-1].start()
        get_momentum[-1].start()
    for copy in first_here:
        copy.wait()

    parts = norm_v[...].astype(jnp.float32)
    values = parts[:, 0, :] + parts[:, 1, :] + parts[:, 2, :]
    lane = lax.broadcasted_iota(jnp.int32, values.shape, 1)
    source = lax.broadcasted_iota(jnp.int32, values.shape, 0)
    paired = jnp.where(
        source % 2 == 0, pltpu.roll(values, owners - 1, 0), pltpu.roll(values, 1, 0)
    )
    pnorm = values + paired
    gnorm = pltpu.roll(values, lanes - row_blocks, 1)
    scale = clip_v[0:1, :] * jnp.sqrt(gnorm) / (jnp.sqrt(pnorm) + epsilon)
    first = me * rows_dev // block_size
    until = (first + 1) * block_size - me * rows_dev
    upper = jnp.sum(jnp.where(lane == first, scale, 0.0), axis=1, keepdims=True)
    lower = jnp.sum(
        jnp.where((lane == first + 1) & (lane < row_blocks), scale, 0.0), axis=1, keepdims=True
    )
    in_upper = lax.broadcasted_iota(jnp.int32, (rows_dev, lanes), 0) < until
    for q in range(pieces):
        get_back[q].wait()
        get_momentum[q].wait()
        for s in range(q * share, (q + 1) * share):
            row_scale = jnp.where(in_upper, upper[s : s + 1], lower[s : s + 1])
            for c in range(columns // lanes):
                at = pl.ds(s * columns + c * lanes, lanes)
                moved = back_v[s, c * rows_dev : (c + 1) * rows_dev, :].astype(jnp.float32)
                momentum_v[:, at] = momentum_rate * momentum_v[:, at] + row_scale * moved
        put_momentum[q].start()
    for copy in put_momentum:
        copy.wait()


def keep_in_hbm(array):
    return pltpu.with_memory_space_constraint(array, pltpu.HBM)


def local(grad, momentum, left_stat, right_stat, left_root, right_root):
    owners = ring_x * ring_z
    place = lax.axis_index("fsdp").astype(jnp.int32).reshape(1)
    rows_dev, all_cols = grad.shape
    row_blocks, _, half, block_size = left_stat.shape
    all_rows = rows_dev * owners
    clip_limit = 0.5 * math.sqrt(all_rows * all_cols)
    length = rows_dev * half // lanes + extra_rows
    smem = pl.BlockSpec(memory_space=pltpu.SMEM)
    in_hbm = pl.BlockSpec(memory_space=pltpu.HBM)
    in_vmem = pl.BlockSpec(memory_space=pltpu.VMEM)
    some_vmem = pltpu.CompilerParams(vmem_limit_bytes=16 << 20)
    flops = row_blocks * 2 * half * block_size * block_size
    dma = pltpu.SemaphoreType.DMA

    def cost(flops, megabytes):
        return pl.CostEstimate(flops=flops, bytes_accessed=megabytes << 20, transcendentals=0)

    def array(*shape, dtype=jnp.bfloat16):
        return jax.ShapeDtypeStruct(shape, dtype)

    left_root = left_root.reshape(row_blocks, half, block_size)
    right_root = right_root.reshape(row_blocks, block_size, half)
    left_stat = left_stat.reshape(row_blocks, half, block_size)
    right_stat = right_stat.reshape(row_blocks, half, block_size)
    group = array(ring_x * rows_dev + extra_rows, block_size)
    stat = array(row_blocks, half, block_size, dtype=jnp.float32)
    wide = array(rows_dev, all_cols, dtype=jnp.float32)
    still = lambda z: 0
    to_partner = outward(-1)

    partner_root = shifted(left_root, 0, to_partner)
    *sent, own = pl.pallas_call(
        cut_kernel,
        out_shape=[group] * roles,
        in_specs=[smem, in_hbm],
        out_specs=[in_vmem] * roles,
        scratch_shapes=[dma((roles * ring_x,))],
        compiler_params=some_vmem,
        cost_estimate=cost(0, 1),
        name="cut",
    )(place, keep_in_hbm(grad))
    far, same, cross = (shifted(block, 0, outward(n)) for block, n in zip(sent, (3, -2, 1)))
    parts = pl.pallas_call(
        pick_kernel,
        out_shape=[group] * ring_x,
        in_specs=[smem] + [in_vmem] * roles + [in_hbm],
        out_specs=[in_vmem] * ring_x,
        compiler_params=some_vmem,
        cost_estimate=cost(0, 2),
        name="pick",
    )(place, far, same, cross, own, partner_root)
    near = [parts[0]] + [shifted(parts[d], d, still) for d in range(1, ring_x)]
    swapped = [shifted(parts[0], 0, to_partner)]
    swapped += [shifted(near[d], 0, to_partner) for d in (1, 2)]
    swapped.append(shifted(parts[3], 3, to_partner))
    roots, right = pl.pallas_call(
        root_kernel,
        out_shape=[
            array(row_blocks, block_size, block_size),
            array(row_blocks, block_size, half),
        ],
        in_specs=[smem] + [in_hbm] * 4,
        out_specs=[in_vmem] * 2,
        scratch_shapes=[dma((3,))],
        compiler_params=some_vmem,
        cost_estimate=cost(0, 4),
        name="roots",
    )(place, keep_in_hbm(left_root), partner_root, keep_in_hbm(right_root), near[2])

    blocks, payload, clip = pl.pallas_call(
        functools.partial(apply_kernel, clip_limit),
        out_shape=[
            array(all_rows, block_size),
            array(owners, length, lanes),
            array(8, lanes, dtype=jnp.float32),
        ],
        in_specs=[smem] + [in_vmem] * (2 * ring_x + 2),
        out_specs=[in_vmem] * 3,
        compiler_params=some_vmem,
        cost_estimate=cost(3 * flops, 6),
        name="apply",
    )(place, *near, *swapped, roots, right)
    back = lax.all_to_all(payload, "fsdp", split_axis=0, concat_axis=0, tiled=True)
    new_left, new_right, clip = pl.pallas_call(
        stat_kernel,
        out_shape=[stat] * 2 + [array(8, lanes, dtype=jnp.float32)],
        in_specs=[smem, in_vmem, in_vmem, in_hbm, in_hbm],
        out_specs=[in_hbm, in_hbm, in_vmem],
        scratch_shapes=[
            pltpu.VMEM((2 * row_blocks, half, block_size), jnp.float32),
            dma((2 * row_blocks,)),
            dma((2 * row_blocks,)),
        ],
        compiler_params=some_vmem,
        cost_estimate=cost(2 * flops, 8),
        name="statistics",
    )(place, clip, blocks, keep_in_hbm(left_stat), keep_in_hbm(right_stat))

    pieces = 8
    new_momentum = pl.pallas_call(
        functools.partial(finish_kernel, row_blocks, block_size),
        out_shape=wide,
        in_specs=[smem] + [in_hbm] * 3,
        out_specs=in_hbm,
        scratch_shapes=[
            pltpu.VMEM((owners, length - extra_rows, lanes), jnp.bfloat16),
            pltpu.VMEM((owners, extra_rows, lanes), jnp.bfloat16),
            pltpu.VMEM((8, lanes), jnp.float32),
            pltpu.VMEM((rows_dev, all_cols), jnp.float32),
            dma((pieces,)),
            dma,
            dma,
            dma((pieces,)),
            dma((pieces,)),
        ],
        compiler_params=some_vmem,
        cost_estimate=cost(1 << 22, 4),
        name="finish",
    )(place, back, clip, keep_in_hbm(momentum))
    shape = (row_blocks, 1, half, block_size)
    return (new_momentum, new_left.reshape(shape), new_right.reshape(shape))


def solution(mesh):
    return jax.shard_map(
        local,
        mesh=mesh,
        in_specs=(
            P(("section", "fsdp"), None),
            P(("section", "fsdp"), None),
            P("section", "fsdp", None, None),
            P("section", "fsdp", None, None),
            P("section", "fsdp", None, None),
            P("section", "fsdp", None, None),
        ),
        out_specs=(
            P(("section", "fsdp"), None),
            P("section", "fsdp", None, None),
            P("section", "fsdp", None, None),
        ),
        check_vma=False,
    )
```
